256 devices in a mesh: rep: 128 (over z, y, x), feat: 2 (over core).
Axes of the slice: x: 4, y: 4, z: 8, core: 2. Of those that a mesh axis runs over, the one named last changes fastest.
Arguments:
- rows: bfloat16 [65536, 768], P('rep', 'feat'), may hold values from -6 to 6
- list_ids: int32 [65536], P('rep'), may hold values from 0 to 16383, as said below
- code_ids: int32 [65536], P('rep'), may hold values from 0 to 4095, as said below
- list_slot: int32 [16384], replicated, may hold values from 0 to 16383, as said below
- coarse: bfloat16 [16384, 768], P('rep'), may hold values from -6 to 6
- codebook: float32 [4096, 768], P(('rep', 'feat')), may hold values from -6 to 6
Outputs:
- updated_codebook: float32 [4096, 768], P(('rep', 'feat'))
- nearest: float32 [65536], P('rep')
The draws below stay inside these ranges and needn't reach their ends.
Inputs may be any that keep to these rules, and one draw needn't show every extreme that they name: A permutation: every slot holds one list; the owner of a list is list_slot // 128. `list_ids`: among the 512 rows of one device, the lists of one owner are named at most 8 times, and exactly 8 times for some owner. `code_ids`: take an owner r of lists and a half f (0 or 1) of the indices of rep; the rows of the devices with rep index in [f * 64, (f + 1) * 64) whose lists r owns name the codewords of any group g (codewords g * 16 up to the next group) at most 2 times, and exactly 2 times for some r, f and g.
All inputs are finite; a program needn't handle non-finite values.
Results may differ from the reference program's by a relative error of at most 0.0013.
The reference program's roundings to bfloat16 on the way (of `residual` and `book`) count: a program that leaves them out, or rounds other values in their place, can miss the bound.
Values may be sent and summed in bfloat16 or wider, within the bound.
A program may use at most 64 MiB of HBM per device.

```python
import jax
import jax.numpy as jnp
from jax import lax

FEATURES = 768
CODES = 4096
ROW_DEV = 512
LIST_DEV = 128
NLISTS = 16384
ROWS = 65536
CAP = 8
CODE_CAP = 2
N_REP = 128
N_FEAT = 2


def slot_table(key):
    return jax.random.permutation(key, NLISTS).astype(jnp.int32)


def owner_plan(key):
    inner = jax.random.fold_in(key, 5)
    owner_key, hot_key, order_key, pick_key = jax.random.split(inner, 4)
    owner_order = jax.random.permutation(owner_key, N_REP).astype(jnp.int32)
    hot_index = jax.random.randint(hot_key, (N_REP,), 0, max(N_REP // 8, 1))
    hot_owner = jnp.take(owner_order, hot_index)
    order_keys = jax.random.split(order_key, N_REP)
    ranks = jax.vmap(lambda k: jax.random.permutation(k, ROW_DEV))(order_keys).astype(jnp.int32)
    spread = (hot_owner[:, None] + 1 + (ranks - CAP) % (N_REP - 1)) % N_REP
    target = jnp.where(ranks < CAP, hot_owner[:, None], spread).astype(jnp.int32)
    within = jax.random.randint(pick_key, (N_REP, ROW_DEV), 0, LIST_DEV)
    return (target, within)


def draw_list_slot(key, part):
    return slot_table(key)


def draw_list_ids(key, part):
    table = slot_table(key)
    inverse = jnp.argsort(table).astype(jnp.int32)
    target, within = owner_plan(key)
    return jnp.take(inverse, target * LIST_DEV + within).reshape(ROWS).astype(jnp.int32)


def draw_code_ids(key, part):
    target, within = owner_plan(key)
    key = jax.random.fold_in(key, 7)
    perm_key, shift_key, code_key = jax.random.split(key, 3)
    devices = N_REP * N_FEAT
    source = jnp.arange(N_REP, dtype=jnp.int32)[:, None] // (N_REP // 2)
    dest = (target * N_FEAT + source).reshape(ROWS).astype(jnp.int32)
    priority = jax.random.permutation(perm_key, ROWS).astype(jnp.int32)
    order = jnp.argsort(dest * ROWS + priority).astype(jnp.int32)
    tally = jnp.sum((dest[:, None] == jnp.arange(devices, dtype=jnp.int32)[None, :]).astype(jnp.int32), axis=0)
    starts = jnp.cumsum(tally) - tally
    sorted_dest = jnp.take(dest, order)
    rank_sorted = jnp.arange(ROWS, dtype=jnp.int32) - jnp.take(starts, sorted_dest)
    rank = jnp.zeros((ROWS,), jnp.int32).at[order].set(rank_sorted.astype(jnp.int32))
    shift = jax.random.randint(shift_key, (devices,), 0, devices).astype(jnp.int32)
    group = (rank // CODE_CAP + jnp.take(shift, dest)) % devices
    code_in = jax.random.randint(code_key, (ROWS,), 0, CODES // devices).astype(jnp.int32)
    return (group * (CODES // devices) + code_in).astype(jnp.int32)


def levels(own_key, shape, cuts, low, top_value):
    factor_of, own = 1.0, jax.random.fold_in(own_key, 6)
    for axis_at, blocks in cuts:
        draws = jnp.exp(jax.random.uniform(jax.random.fold_in(own, axis_at), (blocks,), jnp.float32, low / len(cuts), top_value / len(cuts)))
        factor_of = factor_of * jnp.repeat(draws, shape[axis_at] // blocks).reshape([-1 if axis == axis_at else 1 for axis in range(len(shape))])
    return factor_of


def scatter_about(stream_key, dims, scale, most, pieces=(), kind=jnp.bfloat16):
    drawn = scale * jax.random.normal(stream_key, dims, jnp.float32)
    if pieces:
        drawn = drawn * levels(stream_key, dims, pieces, -0.22, 0.18)
    return jnp.clip(drawn, -most, most).astype(kind)


def setup_inputs(seed: int = 0) -> dict:
    keys = jax.random.split(jax.random.key(seed), 7)
    return {
        "rows": scatter_about(keys[0], (ROWS, FEATURES), 1.0, 6.0, ((0, 128), (1, 2))),
        "list_ids": draw_list_ids(jax.random.fold_in(keys[6], 71), 0),
        "code_ids": draw_code_ids(jax.random.fold_in(keys[6], 71), 0),
        "list_slot": draw_list_slot(jax.random.fold_in(keys[6], 71), 0),
        "coarse": scatter_about(keys[4], (NLISTS, FEATURES), 1.0, 6.0, ((0, 128),)),
        "codebook": scatter_about(keys[5], (CODES, FEATURES), 1.0, 6.0, ((0, 256),), jnp.float32),
    }


prior_weight = 8.0


def reference(rows, list_ids, code_ids, list_slot, coarse, codebook):
    slot = jnp.take(list_slot, list_ids)
    residual = rows.astype(jnp.float32) - jnp.take(coarse, slot, axis=0).astype(jnp.float32)
    res_b = residual.astype(jnp.bfloat16)
    sums = jax.ops.segment_sum(res_b.astype(jnp.float32), code_ids, CODES)
    counts = jax.ops.segment_sum(jnp.ones((ROWS,), jnp.float32), code_ids, CODES)
    updated = (sums + prior_weight * codebook) / (counts[:, None] + prior_weight)
    book = updated.astype(jnp.bfloat16)
    book_norm = jnp.sum(jnp.square(book.astype(jnp.float32)), axis=1)

    def one_block(block):
        row_norm = jnp.sum(jnp.square(block.astype(jnp.float32)), axis=1)
        dots = lax.dot_general(block, book, (((1,), (1,)), ((), ())), preferred_element_type=jnp.float32)
        dist = (row_norm[:, None] - 2.0 * dots + book_norm[None, :]) / FEATURES
        return jnp.min(dist, axis=1)

    nearest = lax.map(one_block, res_b.reshape(N_REP, ROW_DEV, FEATURES)).reshape(ROWS)
    return updated, nearest
```

```python
import jax
import jax.numpy as jnp
from jax import lax
from jax.experimental import pallas as pl
from jax.experimental.pallas import tpu as pltpu
from jax.sharding import PartitionSpec as P

NZ, NY, NX = 8, 4, 4
CHIPS = NZ * NY * NX
FEATURES = 768
HALF = FEATURES // 2
ROWS = 512
CAP = 8
SLOTS = CHIPS * CAP
PRIOR = 8.0
MESH = pl.DeviceIdType.MESH
F32, BF16, I32 = jnp.float32, jnp.bfloat16, jnp.int32
PLANE = NY * NX
CHUNK = PLANE * CAP

ORDERS = ("xyz", "yzx", "zxy")
PART = FEATURES // 3


def iota(shape, axis):
    return lax.broadcasted_iota(I32, shape, axis)


def one_hot(mask):
    return jnp.where(mask, 1.0, 0.0).astype(BF16)


def dot(a, b, over=((1,), (0,))):
    return lax.dot_general(a, b, (over, ((), ())), preferred_element_type=F32)


def split3(v):
    a = v.astype(BF16)
    r = v - a.astype(F32)
    b = r.astype(BF16)
    return a, b, (r - b.astype(F32)).astype(BF16)


def to_message(v):
    v = v.reshape(PLANE, CAP, 2 * PART)
    return jnp.concatenate([v[:, :, :PART], v[:, :, PART:]], axis=1).astype(BF16)


def from_message(m):
    m = m.astype(F32)
    top = m[:, :CAP, :].reshape(CHUNK, PART)
    low = m[:, CAP:, :].reshape(CHUNK, PART)
    return jnp.concatenate([top, low[:, :128]], axis=1), low[:, 128:]


def kernel(
    rows_ref, lid_ref, code_ref, table_ref, coarse_ref, codebook_ref,
    updated_ref, nearest_ref,
    rows_ext, send_a, recv_a, send_b, recv_b, res_ext, res_full, row_rhs,
    sums_own, sums_sib, book_x, book_y, book_z, min_send, min_recv, near_own, near_sib,
    a_send, a_recv, b_send, b_recv, e_send, e_recv, g_send, g_recv, p_send, p_recv,
):
    rep, feat = lax.axis_index("rep"), lax.axis_index("feat")
    z, y, x = rep // PLANE, rep // NX % NY, rep % NX

    def chip(dz, dy, dx):
        return (z + dz) % NZ * PLANE + (y + dy) % NY * NX + (x + dx) % NX

    def ahead(s):
        return (chip(s // PLANE, s // NX % NY, s % NX), feat)

    def behind(s):
        return (chip(NZ - s // PLANE, NY - s // NX % NY, NX - s % NX), feat)

    def nth(i):
        return i % NZ * PLANE + i // NZ

    sibling = (rep, 1 - feat)

    barrier = pltpu.get_barrier_semaphore()

    def greet(s, carry):
        pl.semaphore_signal(barrier, inc=1, device_id=ahead(s), device_id_type=MESH)
        return carry

    lax.fori_loop(1, CHIPS, greet, 0)
    pl.semaphore_signal(barrier, inc=1, device_id=sibling, device_id_type=MESH)

    lid, code = lid_ref[...], code_ref[...]
    table = table_ref[...]
    high = one_hot(iota((128, ROWS), 0) == (lid >> 7))
    low = iota((128, ROWS), 0) == (lid & 127)

    def look_up(t):
        got = dot(t.astype(F32).astype(BF16), high, ((0,), (0,)))
        return jnp.sum(jnp.where(low, got, 0.0), axis=0, keepdims=True)

    owner, local = look_up(table >> 7), look_up(table & 127)
    owner_i = owner.astype(I32)
    rel = (
        (((owner_i >> 4) - z) & (NZ - 1)) * PLANE
        + (((owner_i >> 2) - y) & (NY - 1)) * NX
        + ((owner_i - x) & (NX - 1))
    )
    line = iota((16, ROWS), 0)
    labels = jnp.where(line == 0, local + 1.0, 0.0)
    labels = jnp.where(line == 1, ((code >> 6) + 1).astype(F32), labels)
    labels = jnp.where(line == 2, (code & 63).astype(F32), labels)
    labels = jnp.where(line == 3, owner, labels)
    eye = one_hot(iota((16, 128), 0) == iota((16, 128), 1))
    labels = dot(labels.astype(BF16), eye, ((0,), (0,)))
    rows_ext[:, :HALF] = rows_ref[...]
    rows_ext[:, HALF:] = labels.astype(BF16)
    same = (labels[:, 3:4] == owner) & (iota((ROWS, ROWS), 0) < iota((ROWS, ROWS), 1))
    rank = jnp.sum(jnp.where(same, 1.0, 0.0), axis=0, keepdims=True).astype(I32)
    dest = rel * CAP + rank

    def pack_rows(c, carry):
        pick = one_hot(iota((CHUNK, ROWS), 0) + c * CHUNK == dest)
        send_a[pl.ds(c * PLANE, PLANE)] = to_message(dot(pick, rows_ext[...]))
        return carry

    lax.fori_loop(0, NZ, pack_rows, 0)

    pl.semaphore_wait(barrier, CHIPS)

    def exchange(src, dst, send_sem, recv_sem):
        def start(i, carry):
            s = nth(i)
            pltpu.make_async_remote_copy(
                src_ref=src.at[s], dst_ref=dst.at[s], send_sem=send_sem, recv_sem=recv_sem,
                device_id=ahead(s), device_id_type=MESH,
            ).start()
            return carry

        lax.fori_loop(1, CHIPS, start, 0)
        dst[0] = src[0]

    def others(buf, sem):
        return pltpu.make_async_copy(buf.at[pl.ds(1, CHIPS - 1)], buf.at[pl.ds(1, CHIPS - 1)], sem)

    exchange(send_a, recv_a, a_send, a_recv)
    others(recv_a, a_recv).wait()

    eye_t = eye

    def residuals(c, carry):
        v, tags = from_message(recv_a[pl.ds(c * PLANE, PLANE)])
        pick = one_hot(iota((CHUNK, 128), 1) + 1 == tags[:, 0:1].astype(I32))
        base = dot(pick, coarse_ref[:, pl.ds(pl.multiple_of(feat * HALF, 128), HALF)])
        res = (v - base).astype(BF16)
        at = pl.ds(c * CHUNK, CHUNK)
        res_ext[at, :HALF] = res
        res_ext[at, HALF:] = tags.astype(BF16)
        res_full[feat, at, :] = res
        return carry

    lax.fori_loop(0, NZ, residuals, 0)
    swap_res = pltpu.make_async_remote_copy(
        src_ref=res_full.at[feat], dst_ref=res_full.at[feat], send_sem=p_send.at[0],
        recv_sem=p_recv.at[0], device_id=sibling, device_id_type=MESH,
    )
    swap_res.start()

    tags_t = dot(eye_t, res_ext[:, HALF:], ((1,), (1,)))
    code_i = ((tags_t[1:2] - 1.0) * 64.0 + tags_t[2:3]).astype(I32)
    src_z = (z - iota((1, SLOTS), 1) // CHUNK) & (NZ - 1)
    half = src_z >> 2
    key = jnp.where(code_i >= 0, (code_i >> 4) * 2 + half, -1).astype(F32)

    def count(c, carry):
        at = pl.ds(c * CHUNK, CHUNK)
        tags = res_ext[at, HALF:].astype(F32)
        code_c = ((tags[:, 1:2] - 1.0) * 64.0 + tags[:, 2:3]).astype(I32)
        key_c = ((code_c >> 4) * 2 + (((z - c) & (NZ - 1)) >> 2)).astype(F32)
        before = iota((CHUNK, SLOTS), 0) + c * CHUNK < iota((CHUNK, SLOTS), 1)
        hit = jnp.where((key_c == key) & before, 1.0, 0.0)
        return carry + jnp.sum(hit, axis=0, keepdims=True)

    rank_b = lax.fori_loop(0, NZ, count, jnp.zeros((1, SLOTS), F32)).astype(I32)
    home = code_i >> 5
    rel_b = (
        (((home >> 4) - z) & (NZ - 1)) * PLANE
        + (((home >> 2) - y) & (NY - 1)) * NX
        + ((home - x) & (NX - 1))
    )
    dest_b = rel_b * CAP + ((code_i >> 4) & 1) * 4 + half * 2 + rank_b
    dest_b = jnp.where(code_i >= 0, dest_b, -1)

    def pack_res(c, carry):
        pick = one_hot(iota((CHUNK, SLOTS), 0) + c * CHUNK == dest_b)
        send_b[pl.ds(c * PLANE, PLANE)] = to_message(dot(pick, res_ext[...]))
        return carry

    lax.fori_loop(0, NZ, pack_res, 0)
    exchange(send_b, recv_b, b_send, b_recv)

    swap_res.wait()
    ones = jnp.ones((16, HALF), BF16)
    row_norm = jnp.zeros((16, SLOTS), F32)
    for f in range(2):
        r = res_full[f].astype(F32)
        row_rhs[:, f * HALF : (f + 1) * HALF] = (-2.0 * r).astype(BF16)
        sq = r * r
        sq_hi = sq.astype(BF16)
        sq_lo = (sq - sq_hi.astype(F32)).astype(BF16)
        row_norm += dot(ones, sq_hi, ((1,), (1,))) + dot(ones, sq_lo, ((1,), (1,)))
    row_norm = row_norm[0:1]

    others(recv_b, b_recv).wait()

    def add_up(c, carry):
        sums, counts = carry
        v, tags = from_message(recv_b[pl.ds(c * PLANE, PLANE)])
        t = dot(eye_t, tags.astype(BF16), ((1,), (1,)))
        word = jnp.where(t[1:2] > 0.0, t[2:3], -1.0).astype(I32)
        word = jnp.where(word >= 0, word & 31, -1)
        pick = iota((32, CHUNK), 0) == word
        sums += dot(one_hot(pick), v.astype(BF16))
        counts += jnp.sum(jnp.where(pick, 1.0, 0.0), axis=1, keepdims=True)
        return sums, counts

    sums, counts = lax.fori_loop(
        0, NZ, add_up, (jnp.zeros((32, HALF), F32), jnp.zeros((32, 1), F32))
    )
    sums_own[0], sums_own[1] = sums[:16], sums[16:]
    swap_sums = pltpu.make_async_remote_copy(
        src_ref=sums_own.at[1 - feat], dst_ref=sums_sib, send_sem=p_send.at[1],
        recv_sem=p_recv.at[1], device_id=sibling, device_id_type=MESH,
    )
    swap_sums.start()
    count = jnp.where(feat == 0, counts[:16], counts[16:])
    mine = jnp.where(feat == 0, sums[:16], sums[16:])
    swap_sums.wait()
    theirs = sums_sib[...]
    total = jnp.concatenate(
        [jnp.where(feat == 0, mine, theirs), jnp.where(feat == 0, theirs, mine)], axis=1
    )
    updated = (total + PRIOR * codebook_ref[...]) / (count + PRIOR)
    updated_ref[...] = updated
    book = updated.astype(BF16)

    place, size = {"x": x, "y": y, "z": z}, {"x": NX, "y": NY, "z": NZ}
    bufs = (book_x, book_y, book_z)
    for p, order in enumerate(ORDERS):
        (c1, c2, c3), (n1, n2, _) = [place[a] for a in order], [size[a] for a in order]
        bufs[p][(c3 * n2 + c2) * n1 + c1] = book[:, p * PART : (p + 1) * PART]

    def neighbour(axis, by):
        d = {"x": 0, "y": 0, "z": 0}
        d[axis] = by
        return (chip(d["z"], d["y"], d["x"]), feat)

    steps = []
    for order in ORDERS:
        todo = []
        for phase, axis in enumerate(order):
            todo += [(phase, axis, k) for k in range(size[axis] // 2)]
        steps.append(todo)

    def block(p, phase, origin, part):
        order = ORDERS[p]
        (c1, c2, c3), (n1, n2, _) = [place[a] for a in order], [size[a] for a in order]
        at, n = (
            ((c3 * n2 + c2) * n1 + origin, 1),
            ((c3 * n2 + origin) * n1, n1),
            (origin * n2 * n1, n1 * n2),
        )[phase]
        if part is None:
            return bufs[p].at[pl.ds(at, n)]
        if n == 1:
            return bufs[p].at[pl.ds(at, 1), :, pl.ds(part * 128, 128)]
        return bufs[p].at[pl.ds(at + part * (n // 2), n // 2)]

    moving = [[], [], []]
    sent = []
    for t in range(len(steps[0])):
        for p in range(3):
            for copy in moving[p]:
                copy.wait_recv()
            phase, axis, k = steps[p][t]
            n, c = size[axis], place[axis]
            last = k == n // 2 - 1
            moving[p] = []
            for d, sign in enumerate((1, -1)):
                ref = block(p, phase, (c + n - sign * k) % n, d if last else None)
                moving[p].append(
                    pltpu.make_async_remote_copy(
                        src_ref=ref, dst_ref=ref, send_sem=g_send.at[p, t, d], recv_sem=g_recv.at[p, t, d],
                        device_id=neighbour(axis, sign % n), device_id_type=MESH,
                    )
                )
                moving[p][-1].start()
            sent += moving[p]
    for p in range(3):
        for copy in moving[p]:
            copy.wait_recv()

    def plane(c, best):
        piece_a = book_x[pl.ds(c * PLANE, PLANE)].reshape(256, PART)
        piece_b = jnp.concatenate(
            [book_y[(i % NX * NZ + c) * NY + i // NX] for i in range(PLANE)], axis=0
        )
        piece_c = jnp.concatenate([book_z[i * NZ + c] for i in range(PLANE)], axis=0)
        piece = jnp.concatenate([piece_a, piece_b, piece_c], axis=1)
        f = piece.astype(F32)
        norm = jnp.sum(f * f, axis=1, keepdims=True)
        dist = dot(piece, row_rhs[...], ((1,), (1,))) + norm
        return jnp.minimum(best, jnp.min(dist.reshape(32, 8, SLOTS), axis=0))

    best = lax.fori_loop(0, NZ, plane, jnp.full((8, SLOTS), 3e38, F32))
    best = (jnp.min(best, axis=0, keepdims=True) + row_norm) / FEATURES
    for c in range(NZ):
        min_send[c] = best[:, c * CHUNK : (c + 1) * CHUNK]

    def give_back(i, carry):
        s = nth(i)
        pltpu.make_async_remote_copy(
            src_ref=min_send.at[s // PLANE], dst_ref=min_recv.at[s], send_sem=e_send, recv_sem=e_recv,
            device_id=behind(s), device_id_type=MESH,
        ).start()
        return carry

    lax.fori_loop(1, CHIPS, give_back, 0)
    min_recv[0] = min_send[0]
    others(min_recv, e_recv).wait()
    pick = one_hot(iota((CHIPS, ROWS), 0) == rel)
    got = jnp.zeros((128, ROWS), F32)
    for piece in split3(min_recv[...].reshape(CHIPS, 128)):
        got += dot(piece, pick, ((0,), (0,)))
    lane = (rel & (PLANE - 1)) * CAP + rank
    near = jnp.sum(jnp.where(iota((128, ROWS), 0) == lane, got, 0.0), axis=0, keepdims=True)
    near_own[...] = near
    swap_near = pltpu.make_async_remote_copy(
        src_ref=near_own, dst_ref=near_sib, send_sem=p_send.at[2],
        recv_sem=p_recv.at[2], device_id=sibling, device_id_type=MESH,
    )
    swap_near.start()
    swap_near.wait()
    nearest_ref[...] = jnp.minimum(near, near_sib[...])

    others(send_a, a_send).wait()
    others(send_b, b_send).wait()
    others(min_recv, e_send).wait()
    for copy in sent:
        copy.wait_send()


def per_device(rows, list_ids, code_ids, list_slot, coarse, codebook):
    vmem = pl.BlockSpec(memory_space=pltpu.VMEM)
    message = pltpu.VMEM((CHIPS, 16, PART), BF16)
    dma = pltpu.SemaphoreType.DMA
    updated, nearest = pl.pallas_call(
        kernel,
        out_shape=(
            jax.ShapeDtypeStruct((16, FEATURES), F32),
            jax.ShapeDtypeStruct((1, ROWS), F32),
        ),
        in_specs=[vmem] * 6,
        out_specs=(vmem, vmem),
        scratch_shapes=[
            pltpu.VMEM((ROWS, 512), BF16),
            message, message, message, message,
            pltpu.VMEM((SLOTS, 512), BF16),
            pltpu.VMEM((2, SLOTS, HALF), BF16),
            pltpu.VMEM((SLOTS, FEATURES), BF16),
            pltpu.VMEM((2, 16, HALF), F32),
            pltpu.VMEM((16, HALF), F32),
            message, message, message,
            pltpu.VMEM((NZ, 1, 128), F32),
            pltpu.VMEM((CHIPS, 1, 128), F32),
            pltpu.VMEM((1, ROWS), F32),
            pltpu.VMEM((1, ROWS), F32),
            dma, dma, dma, dma, dma, dma,
            dma((3, 8, 2)), dma((3, 8, 2)), dma((3,)), dma((3,)),
        ],
        compiler_params=pltpu.CompilerParams(
            collective_id=0, has_side_effects=True, vmem_limit_bytes=48 * 2**20
        ),
    )(
        rows,
        list_ids.reshape(1, ROWS),
        code_ids.reshape(1, ROWS),
        list_slot.reshape(128, 128),
        coarse,
        codebook,
    )
    return updated, nearest.reshape(ROWS)


def solution(mesh):
    placed = (P("rep", "feat"), P("rep"), P("rep"), P(), P("rep", None), P(("rep", "feat"), None))
    return jax.shard_map(
        per_device,
        mesh=mesh,
        in_specs=placed,
        out_specs=(P(("rep", "feat"), None), P("rep")),
        check_vma=False,
    )
```

```python
import jax
import jax.numpy as jnp
from jax import lax
from jax.experimental import pallas as pl
from jax.experimental.pallas import tpu as pltpu
from jax.sharding import PartitionSpec as P

NZ, NY, NX = 8, 4, 4
PLANE = NY * NX
CHIPS = NZ * PLANE
FEATURES = 768
HALF = FEATURES // 2
PART = FEATURES // 3
ROWS = 512
CAP = 8
CHUNK = PLANE * CAP
SLOTS = CHIPS * CAP
PRIOR = 8.0
MESH = pl.DeviceIdType.MESH
F32, BF16, I32 = jnp.float32, jnp.bfloat16, jnp.int32
NEAR_FIRST = (0, 1, 7, 2, 6, 3, 5, 4)


def iota(shape, axis):
    return lax.broadcasted_iota(I32, shape, axis)


def one_hot(mask):
    return jnp.where(mask, 1.0, 0.0).astype(BF16)


def dot(a, b, over=((1,), (0,))):
    return lax.dot_general(a, b, (over, ((), ())), preferred_element_type=F32)


def to_messages(v):
    v = v.reshape(PLANE, CAP, HALF)
    return jnp.concatenate([v[:, :, i * 128 : (i + 1) * 128] for i in range(3)], axis=1).astype(BF16)


def from_messages(m):
    m = m.astype(F32)
    return jnp.concatenate(
        [m[:, i * CAP : (i + 1) * CAP, :].reshape(CHUNK, 128) for i in range(3)], axis=1
    )


def kernel(
    rows_hbm, lid_hbm, code_hbm, table_hbm, coarse_hbm, codebook_hbm,
    updated_ref, nearest_ref,
    rows_ref, lid_ref, code_ref, table_ref, coarse_ref, codebook_ref,
    send_a, mid_a, recv_a, send_b, mid_b, recv_b,
    tag_send, tag_mid, tag_recv, pick_b, res_full, row_rhs,
    sums_own, sums_sib, book_a, book_c, book_d, near_own, near_sib,
    load_sem, z_send, z_recv, p_send, p_recv, tag_sem, swap_send, swap_recv,
    t0_send, t0_recv, t1_send, t1_recv, ring_send, ring_recv,
):
    rep, feat = lax.axis_index("rep"), lax.axis_index("feat")
    z, y, x = rep >> 4, (rep >> 2) & 3, rep & 3

    def chip(dz, dy, dx):
        at = (((z + dz) & (NZ - 1)) << 4) | (((y + dy) & 3) << 2) | ((x + dx) & 3)
        return (at, feat)

    def in_plane(p, sign=1):
        return chip(0, sign * (p >> 2), sign * (p & 3))

    sibling = (rep, 1 - feat)

    def remote(src, dst, send_sem, recv_sem, to):
        return pltpu.make_async_remote_copy(
            src_ref=src, dst_ref=dst, send_sem=send_sem, recv_sem=recv_sem,
            device_id=to, device_id_type=MESH,
        )

    def wait_bytes(ref, sem):
        pltpu.make_async_copy(ref, ref, sem).wait()

    loads = [
        pltpu.make_async_copy(src, dst, load_sem.at[i])
        for i, (src, dst) in enumerate(
            (
                (lid_hbm, lid_ref),
                (table_hbm, table_ref),
                (code_hbm, code_ref),
                (rows_hbm, rows_ref),
                (coarse_hbm.at[:, pl.ds(pl.multiple_of(feat * HALF, 128), HALF)], coarse_ref),
                (codebook_hbm, codebook_ref),
            )
        )
    ]
    for load in loads:
        load.start()
    barrier = pltpu.get_barrier_semaphore()
    for p in range(1, PLANE):
        pl.semaphore_signal(barrier, inc=1, device_id=in_plane(p), device_id_type=MESH)
    for dz in range(1, NZ):
        pl.semaphore_signal(barrier, inc=1, device_id=chip(dz, 0, 0), device_id_type=MESH)
    pl.semaphore_signal(barrier, inc=1, device_id=sibling, device_id_type=MESH)

    for load in loads[:3]:
        load.wait()
    lid, code, table = lid_ref[...], code_ref[...], table_ref[...]
    high = one_hot(iota((128, ROWS), 0) == (lid >> 7))
    low = iota((128, ROWS), 0) == (lid & 127)

    def look_up(t):
        got = dot(t.astype(F32).astype(BF16), high, ((0,), (0,)))
        return jnp.sum(jnp.where(low, got, 0.0), axis=0, keepdims=True)

    owner, local = look_up(table >> 7), look_up(table & 127)

    def offset(chip_id):
        return (
            (((chip_id >> 4) - z) & (NZ - 1)) * PLANE
            + (((chip_id >> 2) - y) & (NY - 1)) * NX
            + ((chip_id - x) & (NX - 1))
        )

    def lines(values, width):
        line, out = iota((16, width), 0), jnp.zeros((16, width), F32)
        for i, v in enumerate(values):
            out = jnp.where(line == i, v, out)
        return out.astype(BF16)

    owner_col = dot(lines([owner], ROWS), lines([1.0], ROWS), ((0,), (0,)))
    same = (owner_col == owner) & (iota((ROWS, ROWS), 0) < iota((ROWS, ROWS), 1))
    rank = jnp.sum(jnp.where(same, 1.0, 0.0), axis=0, keepdims=True).astype(I32)
    dest = offset(owner.astype(I32)) * CAP + rank
    tags = lines([local, (code >> 6).astype(F32), (code & 63).astype(F32), 1.0], ROWS)
    loads[3].wait()

    def pack_rows(c, carry):
        pick = one_hot(iota((CHUNK, ROWS), 0) + c * CHUNK == dest)
        send_a[c] = to_messages(dot(pick, rows_ref[...]))
        t = dot(tags, pick, ((1,), (1,)))
        tag_send[0, c] = t[0:1] * 4096.0 + t[1:2] * 64.0 + t[2:3] + t[3:4]
        return carry

    lax.fori_loop(0, NZ, pack_rows, 0)
    loads[4].wait()
    loads[5].wait()
    pl.semaphore_wait(barrier, PLANE + NZ - 1)

    def tags_along_z(n, sign):
        for dz in range(1, NZ):
            remote(tag_send.at[n, dz], tag_mid.at[n, dz], tag_sem.at[n, 0], tag_sem.at[n, 1],
                   chip(sign * dz, 0, 0)).start()
        tag_mid[n, 0] = tag_send[n, 0]

    def tags_in_plane(n, sign):
        wait_bytes(tag_mid.at[n, pl.ds(1, NZ - 1)], tag_sem.at[n, 1])
        for p in range(1, PLANE):
            remote(tag_mid.at[n], tag_recv.at[n, p], tag_sem.at[n, 2], tag_sem.at[n, 3],
                   in_plane(p, sign)).start()
        tag_recv[n, 0] = tag_mid[n]

    def tags_got(n):
        wait_bytes(tag_recv.at[n, pl.ds(1, PLANE - 1)], tag_sem.at[n, 3])
        lane = iota((NZ, 128), 1) >> 3
        out = jnp.zeros((NZ, 128), F32)
        for p in range(PLANE):
            out = jnp.where(lane == p, tag_recv[n, p].reshape(NZ, 128), out)
        return out

    def tags_sent(n):
        wait_bytes(tag_send.at[n, pl.ds(1, NZ - 1)], tag_sem.at[n, 0])
        wait_bytes(tag_recv.at[n, pl.ds(1, PLANE - 1)], tag_sem.at[n, 2])

    def in_a_row(t):
        return jnp.concatenate([t[c : c + 1] for c in range(NZ)], axis=1)

    def along_z(n, src, mid, dz):
        remote(src.at[dz], mid.at[dz], z_send.at[n], z_recv.at[n, dz], chip(dz, 0, 0)).start()

    def forward(n, src, mid, dst, dz):
        held = mid
        if dz == 0:
            held = src
        else:
            wait_bytes(mid.at[dz], z_recv.at[n, dz])

        def start(p, carry):
            remote(held.at[dz, p], dst.at[dz, p], p_send.at[n], p_recv.at[n, dz], in_plane(p)).start()
            return carry

        lax.fori_loop(1, PLANE, start, 0)
        dst[dz, 0] = held[dz, 0]

    def arrived(n, dst, dz):
        wait_bytes(dst.at[dz, pl.ds(1, PLANE - 1)], p_recv.at[n, dz])
        return from_messages(dst[dz])

    def all_sent(n, src, dst):
        wait_bytes(src.at[pl.ds(1, NZ - 1)], z_send.at[n])
        for dz in range(NZ):
            wait_bytes(dst.at[dz, pl.ds(1, PLANE - 1)], p_send.at[n])

    tags_along_z(0, 1)
    for dz in NEAR_FIRST[1:]:
        along_z(0, send_a, mid_a, dz)
    forward(0, send_a, mid_a, recv_a, 0)
    tags_in_plane(0, 1)
    forward(0, send_a, mid_a, recv_a, 1)
    forward(0, send_a, mid_a, recv_a, 7)

    got = in_a_row(tags_got(0)).astype(I32) - 1
    local_b = got >> 12
    code_b = jnp.where(got >= 0, got & 4095, -1)
    half_b = ((z - (iota((1, SLOTS), 1) >> 7)) & (NZ - 1)) >> 2
    key = jnp.where(got >= 0, (code_b >> 4) * 2 + half_b, -1)
    key_f = key.astype(F32)
    key_lines = lines([(key >> 4).astype(F32), (key & 15).astype(F32)], SLOTS)
    weights = lines([16.0, 1.0], SLOTS)
    rank_b = jnp.zeros((1, SLOTS), F32)
    for c in range(NZ):
        key_col = dot(key_lines[:, c * CHUNK : (c + 1) * CHUNK], weights, ((0,), (0,)))
        before = iota((CHUNK, SLOTS), 0) + c * CHUNK < iota((CHUNK, SLOTS), 1)
        hit = jnp.where((key_col == key_f) & before, 1.0, 0.0)
        rank_b += jnp.sum(hit, axis=0, keepdims=True)
    dest_b = offset(code_b >> 5) * CAP + ((code_b >> 4) & 1) * 4 + half_b * 2 + rank_b.astype(I32)
    dest_b = jnp.where(got >= 0, dest_b, -1)
    tags_b = lines([(code_b & 31).astype(F32), 1.0], SLOTS)

    def plan(c, carry):
        pick = one_hot(iota((CHUNK, SLOTS), 0) + c * CHUNK == dest_b)
        pick_b[pl.ds(c * CHUNK, CHUNK), :] = pick
        t = dot(tags_b, pick, ((1,), (1,)))
        tag_send[1, c] = t[0:1] + t[1:2]
        return carry

    lax.fori_loop(0, NZ, plan, 0)
    tags_along_z(1, 1)

    def residual(dz):
        v = arrived(0, recv_a, dz)
        pick = one_hot(iota((128, CHUNK), 0) == local_b[:, dz * CHUNK : (dz + 1) * CHUNK])
        res = (v - dot(pick, coarse_ref[...], ((0,), (0,)))).astype(BF16)
        res_full[feat, pl.ds(dz * CHUNK, CHUNK), :] = res

    forward(0, send_a, mid_a, recv_a, 2)
    forward(0, send_a, mid_a, recv_a, 6)
    residual(0)
    residual(1)
    residual(7)
    tags_in_plane(1, 1)
    forward(0, send_a, mid_a, recv_a, 3)
    forward(0, send_a, mid_a, recv_a, 5)
    residual(2)
    residual(6)
    forward(0, send_a, mid_a, recv_a, 4)
    residual(3)
    residual(5)
    residual(4)

    for dz in NEAR_FIRST[1:] + (0,):
        pick = pick_b[dz * CHUNK : (dz + 1) * CHUNK, :]
        send_b[dz] = to_messages(dot(pick, res_full[feat]))
        if dz:
            along_z(1, send_b, mid_b, dz)
    swap_res = remote(res_full.at[feat], res_full.at[feat], swap_send.at[0], swap_recv.at[0], sibling)
    swap_res.start()
    forward(1, send_b, mid_b, recv_b, 0)
    word = in_a_row(tags_got(1)).astype(I32) - 1
    forward(1, send_b, mid_b, recv_b, 1)
    forward(1, send_b, mid_b, recv_b, 7)

    swap_res.wait()
    ones = jnp.ones((16, HALF), BF16)
    row_norm = jnp.zeros((16, SLOTS), F32)
    for f in range(2):
        r = res_full[f].astype(F32)
        row_rhs[:, f * HALF : (f + 1) * HALF] = (-2.0 * r).astype(BF16)
        sq = r * r
        sq_hi = sq.astype(BF16)
        sq_lo = (sq - sq_hi.astype(F32)).astype(BF16)
        row_norm += dot(ones, sq_hi, ((1,), (1,))) + dot(ones, sq_lo, ((1,), (1,)))
    row_norm = row_norm[0:1]

    sums, counts = jnp.zeros((32, HALF), F32), jnp.zeros((32, 1), F32)

    def add_up(dz, sums, counts):
        v = arrived(1, recv_b, dz).astype(BF16)
        pick = iota((32, CHUNK), 0) == word[:, dz * CHUNK : (dz + 1) * CHUNK]
        counts += jnp.sum(jnp.where(pick, 1.0, 0.0), axis=1, keepdims=True)
        return sums + dot(one_hot(pick), v), counts

    forward(1, send_b, mid_b, recv_b, 2)
    forward(1, send_b, mid_b, recv_b, 6)
    for dz in (0, 1, 7):
        sums, counts = add_up(dz, sums, counts)
    forward(1, send_b, mid_b, recv_b, 3)
    forward(1, send_b, mid_b, recv_b, 5)
    for dz in (2, 6):
        sums, counts = add_up(dz, sums, counts)
    forward(1, send_b, mid_b, recv_b, 4)
    for dz in (3, 5, 4):
        sums, counts = add_up(dz, sums, counts)
    sums_own[0], sums_own[1] = sums[:16], sums[16:]
    swap_sums = remote(sums_own.at[1 - feat], sums_sib, swap_send.at[1], swap_recv.at[1], sibling)
    swap_sums.start()
    count = jnp.where(feat == 0, counts[:16], counts[16:])
    mine = jnp.where(feat == 0, sums[:16], sums[16:])
    swap_sums.wait()
    theirs = sums_sib[...]
    total = jnp.concatenate(
        [jnp.where(feat == 0, mine, theirs), jnp.where(feat == 0, theirs, mine)], axis=1
    )
    updated = (total + PRIOR * codebook_ref[...]) / (count + PRIOR)
    updated_ref[...] = updated
    book = updated.astype(BF16)

    at_a, at_c, at_d = (z * NY + y) * NX + x, (y * NX + x) * NZ + z, (x * NY + y) * NZ + z
    book_a[at_a] = book[:, :PART]
    book_c[at_c] = book[:, PART : 2 * PART]
    book_d[at_d] = book[:, 2 * PART :]
    for dz in range(1, NZ):
        for i, (buf, at) in enumerate(((book_c, at_c), (book_d, at_d))):
            remote(buf.at[at], buf.at[at], t0_send.at[i], t0_recv.at[i], chip(dz, 0, 0)).start()
    for p in range(1, PLANE):
        remote(book_a.at[at_a], book_a.at[at_a], t0_send.at[2], t0_recv.at[2], in_plane(p)).start()

    sent = []

    def ring(n, buf, place, size, block, step, k):
        half = block // 2
        copies = []
        for d, sign in enumerate((1, -1)):
            at = ((place - sign * k) & (size - 1)) * block
            ref = buf.at[pl.ds(at, block)]
            if k == size // 2 - 1:
                ref = buf.at[pl.ds(at + d * half, half)]
            to = chip(*(sign * s for s in step))
            copies.append(remote(ref, ref, ring_send.at[n, k, d], ring_recv.at[n, k, d], to))
        for copy in copies:
            copy.start()
        sent.extend(copies)
        return copies

    def came(copies):
        for copy in copies:
            copy.wait_recv()

    def ring_a(k):
        return ring(0, book_a, z, NZ, PLANE, (1, 0, 0), k)

    def ring_c(k):
        return ring(1, book_c, y, NY, NX * NZ, (0, 1, 0), k)

    def ring_d(k):
        return ring(2, book_d, x, NX, NY * NZ, (0, 0, 1), k)

    wait_bytes(book_c.at[pl.ds(0, NZ - 1)], t0_recv.at[0])
    wait_bytes(book_d.at[pl.ds(0, NZ - 1)], t0_recv.at[1])
    line_c = book_c.at[pl.ds((y * NX + x) * NZ, NZ)]
    line_d = book_d.at[pl.ds((x * NY + y) * NZ, NZ)]
    for i in range(1, NX):
        remote(line_c, line_c, t1_send.at[0], t1_recv.at[0], chip(0, 0, i)).start()
        remote(line_d, line_d, t1_send.at[1], t1_recv.at[1], chip(0, i, 0)).start()
    wait_bytes(book_a.at[pl.ds(0, PLANE - 1)], t0_recv.at[2])
    a0 = ring_a(0)
    wait_bytes(book_c.at[pl.ds(0, 3 * NZ)], t1_recv.at[0])
    c0 = ring_c(0)
    wait_bytes(book_d.at[pl.ds(0, 3 * NZ)], t1_recv.at[1])
    d0 = ring_d(0)
    came(a0)
    a1 = ring_a(1)
    came(c0)
    c1 = ring_c(1)
    came(d0)
    d1 = ring_d(1)
    came(a1)
    a2 = ring_a(2)
    came(a2)
    a3 = ring_a(3)
    came(c1)
    came(d1)
    came(a3)

    def book_sent():
        for i, (buf, n) in enumerate(((book_c, NZ - 1), (book_d, NZ - 1), (book_a, PLANE - 1))):
            wait_bytes(buf.at[pl.ds(0, n)], t0_send.at[i])
        for i, buf in enumerate((book_c, book_d)):
            wait_bytes(buf.at[pl.ds(0, 3 * NZ)], t1_send.at[i])
        for copy in sent:
            copy.wait_send()


    def plane(c, best):
        piece_a = book_a[pl.ds(c * PLANE, PLANE)].reshape(256, PART)
        piece_c = jnp.concatenate([book_c[i * NZ + c] for i in range(PLANE)], axis=0)
        piece_d = jnp.concatenate(
            [book_d[(i % NX * NY + i // NX) * NZ + c] for i in range(PLANE)], axis=0
        )
        piece = jnp.concatenate([piece_a, piece_c, piece_d], axis=1)
        f = piece.astype(F32)
        norm = jnp.sum(f * f, axis=1, keepdims=True)
        dist = dot(piece, row_rhs[...], ((1,), (1,))) + norm
        return jnp.minimum(best, jnp.min(dist.reshape(32, 8, SLOTS), axis=0))

    best = lax.fori_loop(0, NZ, plane, jnp.full((8, SLOTS), 3e38, F32))
    best = (jnp.min(best, axis=0, keepdims=True) + row_norm) / FEATURES
    for c in range(NZ):
        tag_send[2, c] = best[:, c * CHUNK : (c + 1) * CHUNK]

    tags_along_z(2, -1)
    tags_in_plane(2, -1)
    back = tags_got(2)
    parts = []
    for _ in range(3):
        parts.append(back.astype(BF16).astype(F32))
        back = back - parts[-1]
    lane = one_hot(iota((128, ROWS), 0) == (dest & 127))
    near = dot(jnp.concatenate(parts, axis=0).astype(BF16), lane)
    near = near[:8] + near[8:16] + near[16:]
    near = jnp.sum(jnp.where(iota((NZ, ROWS), 0) == (dest >> 7), near, 0.0), axis=0, keepdims=True)
    near_own[...] = near
    swap_near = remote(near_own, near_sib, swap_send.at[2], swap_recv.at[2], sibling)
    swap_near.start()

    for n in range(3):
        tags_sent(n)
    all_sent(0, send_a, recv_a)
    all_sent(1, send_b, recv_b)
    book_sent()
    swap_near.wait()
    nearest_ref[...] = jnp.minimum(near, near_sib[...])


def per_device(rows, list_ids, code_ids, list_slot, coarse, codebook):
    vmem, hbm = pl.BlockSpec(memory_space=pltpu.VMEM), pl.BlockSpec(memory_space=pl.ANY)
    messages = pltpu.VMEM((NZ, PLANE, 24, 128), BF16)
    blocks = pltpu.VMEM((CHIPS, 16, PART), BF16)
    dma = pltpu.SemaphoreType.DMA
    updated, nearest = pl.pallas_call(
        kernel,
        out_shape=(
            jax.ShapeDtypeStruct((16, FEATURES), F32),
            jax.ShapeDtypeStruct((1, ROWS), F32),
        ),
        in_specs=[hbm] * 6,
        out_specs=(vmem, vmem),
        scratch_shapes=[
            pltpu.VMEM((ROWS, HALF), BF16),
            pltpu.VMEM((1, ROWS), I32),
            pltpu.VMEM((1, ROWS), I32),
            pltpu.VMEM((128, 128), I32),
            pltpu.VMEM((128, HALF), BF16),
            pltpu.VMEM((16, FEATURES), F32),
            messages, messages, messages, messages, messages, messages,
            pltpu.VMEM((3, NZ, 1, 128), F32),
            pltpu.VMEM((3, NZ, 1, 128), F32),
            pltpu.VMEM((3, PLANE, NZ, 1, 128), F32),
            pltpu.VMEM((SLOTS, SLOTS), BF16),
            pltpu.VMEM((2, SLOTS, HALF), BF16),
            pltpu.VMEM((SLOTS, FEATURES), BF16),
            pltpu.VMEM((2, 16, HALF), F32),
            pltpu.VMEM((16, HALF), F32),
            blocks, blocks, blocks,
            pltpu.VMEM((1, ROWS), F32),
            pltpu.VMEM((1, ROWS), F32),
            dma((6,)), dma((2,)), dma((2, NZ)), dma((2,)), dma((2, NZ)), dma((3, 4)), dma((3,)), dma((3,)),
            dma((3,)), dma((3,)), dma((2,)), dma((2,)), dma((3, 4, 2)), dma((3, 4, 2)),
        ],
        compiler_params=pltpu.CompilerParams(
            collective_id=0, has_side_effects=True, vmem_limit_bytes=63 * 2**20
        ),
    )(
        rows,
        list_ids.reshape(1, ROWS),
        code_ids.reshape(1, ROWS),
        list_slot.reshape(128, 128),
        coarse,
        codebook,
    )
    return updated, nearest.reshape(ROWS)


def solution(mesh):
    placed = (P("rep", "feat"), P("rep"), P("rep"), P(), P("rep", None), P(("rep", "feat"), None))
    return jax.shard_map(
        per_device,
        mesh=mesh,
        in_specs=placed,
        out_specs=(P(("rep", "feat"), None), P("rep")),
        check_vma=False,
    )
```

```python
import jax
import jax.numpy as jnp
from jax import lax
from jax.experimental import pallas as pl
from jax.experimental.pallas import tpu as pltpu
from jax.sharding import PartitionSpec as P

NZ, NY, NX = 8, 4, 4
PLANE = NY * NX
CHIPS = NZ * PLANE
FEATURES = 768
HALF = FEATURES // 2
PART = FEATURES // 3
ROWS = 512
CAP = 8
CHUNK = PLANE * CAP
SLOTS = CHIPS * CAP
PRIOR = 8.0
MESH = pl.DeviceIdType.MESH
F32, BF16, I32 = jnp.float32, jnp.bfloat16, jnp.int32
SLAB = 4 * NZ
PARTS = 3


def iota(shape, axis):
    return lax.broadcasted_iota(I32, shape, axis)


def one_hot(mask):
    return jnp.where(mask, 1.0, 0.0).astype(BF16)


def dot(a, b, over=((1,), (0,))):
    return lax.dot_general(a, b, (over, ((), ())), preferred_element_type=F32)


def kernel(
    rows_hbm, lid_hbm, code_hbm, table_hbm, coarse_hbm, codebook_hbm,
    updated_ref, nearest_ref,
    rows_ref, lid_ref, code_ref, table_ref, coarse_ref, codebook_ref,
    send_a, mid_a, recv_a, send_b, mid_b, recv_b,
    tag_send, tag_mid, tag_recv, pick_b, base_ref, res_full, row_rhs, acc_ref,
    sums_own, sums_sib, books, near_own, near_sib,
    load_sem, z_send, z_recv, p_send, p_recv, tag_sem, swap_send, swap_recv, g_send, g_recv, r_send, r_recv,
):
    rep, feat = lax.axis_index("rep"), lax.axis_index("feat")
    z, y, x = rep >> 4, (rep >> 2) & 3, rep & 3

    def chip(dz, dy, dx):
        at = (((z + dz) & (NZ - 1)) << 4) | (((y + dy) & 3) << 2) | ((x + dx) & 3)
        return (at, feat)

    def in_plane(p, sign=1):
        return chip(0, sign * (p >> 2), sign * (p & 3))

    sibling = (rep, 1 - feat)

    def remote(src, dst, send_sem, recv_sem, to):
        return pltpu.make_async_remote_copy(
            src_ref=src, dst_ref=dst, send_sem=send_sem, recv_sem=recv_sem,
            device_id=to, device_id_type=MESH,
        )

    def wait_bytes(ref, sem):
        pltpu.make_async_copy(ref, ref, sem).wait()

    loads = [
        pltpu.make_async_copy(src, dst, load_sem.at[i])
        for i, (src, dst) in enumerate(
            (
                (lid_hbm, lid_ref),
                (table_hbm, table_ref),
                (code_hbm, code_ref),
                (rows_hbm, rows_ref),
                (coarse_hbm.at[:, pl.ds(pl.multiple_of(feat * HALF, 128), HALF)], coarse_ref),
                (codebook_hbm, codebook_ref),
            )
        )
    ]
    for load in loads:
        load.start()
    barrier = pltpu.get_barrier_semaphore()
    for p in range(1, PLANE):
        pl.semaphore_signal(barrier, inc=1, device_id=in_plane(p), device_id_type=MESH)
    for dz in range(1, NZ):
        pl.semaphore_signal(barrier, inc=1, device_id=chip(dz, 0, 0), device_id_type=MESH)
    pl.semaphore_signal(barrier, inc=1, device_id=sibling, device_id_type=MESH)

    for load in loads[:3]:
        load.wait()
    lid, code, table = lid_ref[...], code_ref[...], table_ref[...]
    high = one_hot(iota((128, ROWS), 0) == (lid >> 7))
    low = iota((128, ROWS), 0) == (lid & 127)

    def look_up(t):
        got = dot(t.astype(F32).astype(BF16), high, ((0,), (0,)))
        return jnp.sum(jnp.where(low, got, 0.0), axis=0, keepdims=True)

    owner, local = look_up(table >> 7), look_up(table & 127)

    def offset(chip_id):
        return (
            (((chip_id >> 4) - z) & (NZ - 1)) * PLANE
            + (((chip_id >> 2) - y) & (NY - 1)) * NX
            + ((chip_id - x) & (NX - 1))
        )

    def lines(values, width):
        line, out = iota((16, width), 0), jnp.zeros((16, width), F32)
        for i, v in enumerate(values):
            out = jnp.where(line == i, v, out)
        return out.astype(BF16)

    owner_col = dot(lines([owner], ROWS), lines([1.0], ROWS), ((0,), (0,)))
    same = (owner_col == owner) & (iota((ROWS, ROWS), 0) < iota((ROWS, ROWS), 1))
    rank = jnp.sum(jnp.where(same, 1.0, 0.0), axis=0, keepdims=True).astype(I32)
    dest = offset(owner.astype(I32)) * CAP + rank
    tags = lines([local, (code >> 6).astype(F32), (code & 63).astype(F32), 1.0], ROWS)
    loads[3].wait()

    def pack_rows(c, carry):
        pick = one_hot(iota((CHUNK, ROWS), 0) + c * CHUNK == dest)
        out = dot(pick, rows_ref[...])
        for i in range(PARTS):
            send_a[i, c] = out[:, i * 128 : (i + 1) * 128].reshape(PLANE, CAP, 128).astype(BF16)
        t = dot(tags, pick, ((1,), (1,)))
        tag_send[0, c] = t[0:1] * 4096.0 + t[1:2] * 64.0 + t[2:3] + t[3:4]
        return carry

    lax.fori_loop(0, NZ, pack_rows, 0)
    loads[4].wait()
    loads[5].wait()
    pl.semaphore_wait(barrier, PLANE + NZ - 1)

    def tags_along_z(n, sign):
        for dz in range(1, NZ):
            remote(tag_send.at[n, dz], tag_mid.at[n, dz], tag_sem.at[n, 0], tag_sem.at[n, 1],
                   chip(sign * dz, 0, 0)).start()
        tag_mid[n, 0] = tag_send[n, 0]

    def tags_in_plane(n, sign):
        wait_bytes(tag_mid.at[n, pl.ds(1, NZ - 1)], tag_sem.at[n, 1])
        for p in range(1, PLANE):
            remote(tag_mid.at[n], tag_recv.at[n, p], tag_sem.at[n, 2], tag_sem.at[n, 3],
                   in_plane(p, sign)).start()
        tag_recv[n, 0] = tag_mid[n]

    def tags_got(n):
        wait_bytes(tag_recv.at[n, pl.ds(1, PLANE - 1)], tag_sem.at[n, 3])
        lane = iota((NZ, 128), 1) >> 3
        out = jnp.zeros((NZ, 128), F32)
        for p in range(PLANE):
            out = jnp.where(lane == p, tag_recv[n, p].reshape(NZ, 128), out)
        return out

    def tags_sent(n):
        wait_bytes(tag_send.at[n, pl.ds(1, NZ - 1)], tag_sem.at[n, 0])
        wait_bytes(tag_recv.at[n, pl.ds(1, PLANE - 1)], tag_sem.at[n, 2])

    def in_a_row(t):
        return jnp.concatenate([t[c : c + 1] for c in range(NZ)], axis=1)

    def along_z(n, src, mid, i):
        for dz in (4, 3, 5, 2, 6, 1, 7):
            remote(src.at[i, dz], mid.at[i, dz], z_send.at[n], z_recv.at[n, i], chip(dz, 0, 0)).start()
        mid[i, 0] = src[i, 0]

    def forward(n, mid, dst, i):
        wait_bytes(mid.at[i, pl.ds(1, NZ - 1)], z_recv.at[n, i])
        for p in range(1, PLANE):
            remote(mid.at[i, :, p], dst.at[i, :, p], p_send.at[n], p_recv.at[n, i], in_plane(p)).start()
        dst[i, :, 0] = mid[i, :, 0]

    def arrived(n, dst, i):
        wait_bytes(dst.at[i, :, pl.ds(1, PLANE - 1)], p_recv.at[n, i])
        return dst[i].astype(F32).reshape(SLOTS, 128)

    def all_sent(n, src, dst):
        for i in range(PARTS):
            wait_bytes(src.at[i, pl.ds(1, NZ - 1)], z_send.at[n])
            wait_bytes(dst.at[i, :, pl.ds(1, PLANE - 1)], p_send.at[n])

    tags_along_z(0, 1)
    for i in range(PARTS):
        along_z(0, send_a, mid_a, i)
    tags_in_plane(0, 1)
    forward(0, mid_a, recv_a, 0)

    got = in_a_row(tags_got(0)).astype(I32) - 1
    local_b = got >> 12
    code_b = jnp.where(got >= 0, got & 4095, -1)
    half_b = ((z - (iota((1, SLOTS), 1) >> 7)) & (NZ - 1)) >> 2
    key = jnp.where(got >= 0, (code_b >> 4) * 2 + half_b, -1)
    key_f = key.astype(F32)
    key_lines = lines([(key >> 4).astype(F32), (key & 15).astype(F32)], SLOTS)
    weights = lines([16.0, 1.0], SLOTS)
    rank_b = jnp.zeros((1, SLOTS), F32)
    for c in range(NZ):
        key_col = dot(key_lines[:, c * CHUNK : (c + 1) * CHUNK], weights, ((0,), (0,)))
        before = iota((CHUNK, SLOTS), 0) + c * CHUNK < iota((CHUNK, SLOTS), 1)
        hit = jnp.where((key_col == key_f) & before, 1.0, 0.0)
        rank_b += jnp.sum(hit, axis=0, keepdims=True)
    dest_b = offset(code_b >> 5) * CAP + ((code_b >> 4) & 1) * 4 + half_b * 2 + rank_b.astype(I32)
    dest_b = jnp.where(got >= 0, dest_b, -1)
    tags_b = lines([(code_b & 31).astype(F32), 1.0], SLOTS)

    def plan(c, carry):
        pick = one_hot(iota((CHUNK, SLOTS), 0) + c * CHUNK == dest_b)
        pick_b[pl.ds(c * CHUNK, CHUNK), :] = pick
        t = dot(tags_b, pick, ((1,), (1,)))
        tag_send[1, c] = t[0:1] + t[1:2]
        return carry

    lax.fori_loop(0, NZ, plan, 0)
    tags_along_z(1, 1)
    for c in range(NZ):
        pick = one_hot(iota((128, CHUNK), 0) == local_b[:, c * CHUNK : (c + 1) * CHUNK])
        base = dot(pick, coarse_ref[...], ((0,), (0,)))
        base_ref[c * CHUNK : (c + 1) * CHUNK, :] = base.astype(BF16)

    def residual(i):
        at = slice(i * 128, (i + 1) * 128)
        res = (arrived(0, recv_a, i) - base_ref[:, at].astype(F32)).astype(BF16)
        res_full[feat, :, at] = res
        send_b[i] = dot(pick_b[...], res).reshape(NZ, PLANE, CAP, 128).astype(BF16)
        along_z(1, send_b, mid_b, i)

    forward(0, mid_a, recv_a, 1)
    residual(0)
    forward(0, mid_a, recv_a, 2)
    tags_in_plane(1, 1)
    residual(1)
    residual(2)
    swap_res = remote(res_full.at[feat], res_full.at[feat], swap_send.at[0], swap_recv.at[0], sibling)
    swap_res.start()
    forward(1, mid_b, recv_b, 0)

    word = in_a_row(tags_got(1)).astype(I32) - 1
    named = iota((32, SLOTS), 0) == word
    counts = jnp.sum(jnp.where(named, 1.0, 0.0), axis=1, keepdims=True)
    count = jnp.where(feat == 0, counts[:16], counts[16:])
    named = one_hot(named)

    def order(b):
        first, last = ((x, y), (y, x))[b % 2]
        line = (last * 4 + first) * NZ
        return line + z, line, last

    def on(axis, i):
        return chip(0, i, 0) if axis == 0 else chip(0, 0, i)

    def gather_z(b, block):
        at, _, _ = order(b)
        books[b, at] = block
        ref = books.at[b, at]
        for dz in range(1, NZ):
            remote(ref, ref, g_send.at[b, 0], g_recv.at[b, 0], chip(dz, 0, 0)).start()

    def some(b, n):
        return books.at[b, pl.ds(0, n)]

    def gather_line(b):
        wait_bytes(some(b, NZ - 1), g_recv.at[b, 0])
        _, line, _ = order(b)
        ref = books.at[b, pl.ds(line, NZ)]
        for i in (2, 1, 3):
            remote(ref, ref, g_send.at[b, 1], g_recv.at[b, 1], on(1 - b % 2, i)).start()

    def ring(b, k):
        _, _, last = order(b)
        for d, i in enumerate((1, 3)):
            if k == 0:
                ref = books.at[b, pl.ds(last * SLAB, SLAB)]
            else:
                ref = books.at[b, pl.ds(((last - i) & 3) * SLAB + d * (SLAB // 2), SLAB // 2)]
            remote(ref, ref, r_send.at[b, k, d], r_recv.at[b, k, d], on(b % 2, i)).start()

    def gather_ring(b):
        wait_bytes(some(b, 3 * NZ), g_recv.at[b, 1])
        ring(b, 0)

    def ring_came(b, k):
        for d in range(2):
            wait_bytes(some(b, SLAB >> k), r_recv.at[b, k, d])

    def gather_on(b):
        ring_came(b, 0)
        ring(b, 1)

    def both(do, i):
        do(2 * i)
        do(2 * i + 1)

    def update(i):
        sums = dot(named, arrived(1, recv_b, i).astype(BF16))
        sums_own[i, 0], sums_own[i, 1] = sums[:16], sums[16:]
        swap = remote(sums_own.at[i, 1 - feat], sums_sib.at[i], swap_send.at[1 + i], swap_recv.at[1 + i], sibling)
        swap.start()
        mine = jnp.where(feat == 0, sums[:16], sums[16:])
        swap.wait()
        theirs = sums_sib[i]
        block = []
        for f in range(2):
            at = slice(f * HALF + i * 128, f * HALF + (i + 1) * 128)
            total = jnp.where(feat == f, mine, theirs)
            new = (total + PRIOR * codebook_ref[:, at]) / (count + PRIOR)
            updated_ref[:, at] = new
            block.append(new.astype(BF16))
        for f in range(2):
            gather_z(2 * i + f, block[f])

    def rows_side():
        swap_res.wait()
        ones = jnp.ones((16, HALF), BF16)
        norm = jnp.zeros((16, SLOTS), F32)
        for f in range(2):
            r = res_full[f].astype(F32)
            for i in range(PARTS):
                at = i * 2 + f
                row_rhs[:, at * 128 : (at + 1) * 128] = (-2.0 * r[:, i * 128 : (i + 1) * 128]).astype(BF16)
            sq = r * r
            sq_hi = sq.astype(BF16)
            sq_lo = (sq - sq_hi.astype(F32)).astype(BF16)
            norm += dot(ones, sq_hi, ((1,), (1,))) + dot(ones, sq_lo, ((1,), (1,)))
        return norm[0:1]

    forward(1, mid_b, recv_b, 1)
    update(0)
    row_norm = rows_side()
    forward(1, mid_b, recv_b, 2)
    both(gather_line, 0)
    update(1)
    both(gather_ring, 0)
    both(gather_line, 1)
    update(2)
    both(gather_ring, 1)
    both(gather_on, 0)
    both(gather_line, 2)
    both(gather_on, 1)
    both(gather_ring, 2)
    both(lambda b: ring_came(b, 1), 0)
    both(lambda b: ring_came(b, 1), 1)

    def blocks(b, c):
        at = [i if b % 2 == 0 else i % 4 * 4 + i // 4 for i in range(PLANE)]
        return jnp.concatenate([books[b, i * NZ + c] for i in at], axis=0)

    def products(c, pieces):
        piece = jnp.concatenate([blocks(b, c) for b in pieces], axis=1)
        f = piece.astype(F32)
        at = slice(pieces[0] * 128, (pieces[-1] + 1) * 128)
        return dot(piece, row_rhs[:, at], ((1,), (1,))) + jnp.sum(f * f, axis=1, keepdims=True)

    def begin(c, carry):
        acc_ref[c] = products(c, (0, 1, 2, 3))
        return carry

    lax.fori_loop(0, NZ, begin, 0)
    both(gather_on, 2)
    both(lambda b: ring_came(b, 1), 2)

    def book_sent():
        for b in range(2 * PARTS):
            wait_bytes(some(b, NZ - 1), g_send.at[b, 0])
            wait_bytes(some(b, 3 * NZ), g_send.at[b, 1])
            for k in range(2):
                for d in range(2):
                    wait_bytes(some(b, SLAB >> k), r_send.at[b, k, d])


    def finish(c, best):
        dist = acc_ref[c] + products(c, (4, 5))
        return jnp.minimum(best, jnp.min(dist.reshape(32, 8, SLOTS), axis=0))

    best = lax.fori_loop(0, NZ, finish, jnp.full((8, SLOTS), 3e38, F32))
    best = (jnp.min(best, axis=0, keepdims=True) + row_norm) / FEATURES
    for c in range(NZ):
        tag_send[2, c] = best[:, c * CHUNK : (c + 1) * CHUNK]

    tags_along_z(2, -1)
    tags_in_plane(2, -1)
    back = tags_got(2)
    parts = []
    for _ in range(3):
        parts.append(back.astype(BF16).astype(F32))
        back = back - parts[-1]
    lane = one_hot(iota((128, ROWS), 0) == (dest & 127))
    near = dot(jnp.concatenate(parts, axis=0).astype(BF16), lane)
    near = near[:8] + near[8:16] + near[16:]
    near = jnp.sum(jnp.where(iota((NZ, ROWS), 0) == (dest >> 7), near, 0.0), axis=0, keepdims=True)
    near_own[...] = near
    swap_near = remote(near_own, near_sib, swap_send.at[4], swap_recv.at[4], sibling)
    swap_near.start()

    for n in range(3):
        tags_sent(n)
    all_sent(0, send_a, recv_a)
    all_sent(1, send_b, recv_b)
    book_sent()
    swap_near.wait()
    nearest_ref[...] = jnp.minimum(near, near_sib[...])


def per_device(rows, list_ids, code_ids, list_slot, coarse, codebook):
    vmem, hbm = pl.BlockSpec(memory_space=pltpu.VMEM), pl.BlockSpec(memory_space=pl.ANY)
    messages = pltpu.VMEM((PARTS, NZ, PLANE, CAP, 128), BF16)
    dma = pltpu.SemaphoreType.DMA
    updated, nearest = pl.pallas_call(
        kernel,
        out_shape=(
            jax.ShapeDtypeStruct((16, FEATURES), F32),
            jax.ShapeDtypeStruct((1, ROWS), F32),
        ),
        in_specs=[hbm] * 6,
        out_specs=(vmem, vmem),
        scratch_shapes=[
            pltpu.VMEM((ROWS, HALF), BF16),
            pltpu.VMEM((1, ROWS), I32),
            pltpu.VMEM((1, ROWS), I32),
            pltpu.VMEM((128, 128), I32),
            pltpu.VMEM((128, HALF), BF16),
            pltpu.VMEM((16, FEATURES), F32),
            messages, messages, messages, messages, messages, messages,
            pltpu.VMEM((3, NZ, 1, 128), F32),
            pltpu.VMEM((3, NZ, 1, 128), F32),
            pltpu.VMEM((3, PLANE, NZ, 1, 128), F32),
            pltpu.VMEM((SLOTS, SLOTS), BF16),
            pltpu.VMEM((SLOTS, HALF), BF16),
            pltpu.VMEM((2, SLOTS, HALF), BF16),
            pltpu.VMEM((SLOTS, FEATURES), BF16),
            pltpu.VMEM((NZ, 256, SLOTS), F32),
            pltpu.VMEM((PARTS, 2, 16, 128), F32),
            pltpu.VMEM((PARTS, 16, 128), F32),
            pltpu.VMEM((2 * PARTS, CHIPS, 16, 128), BF16),
            pltpu.VMEM((1, ROWS), F32),
            pltpu.VMEM((1, ROWS), F32),
            dma((6,)), dma((2,)), dma((2, PARTS)), dma((2,)), dma((2, PARTS)), dma((3, 4)), dma((5,)), dma((5,)),
            dma((6, 2)), dma((6, 2)), dma((6, 2, 2)), dma((6, 2, 2)),
        ],
        compiler_params=pltpu.CompilerParams(
            collective_id=0, has_side_effects=True, vmem_limit_bytes=63 * 2**20
        ),
    )(
        rows,
        list_ids.reshape(1, ROWS),
        code_ids.reshape(1, ROWS),
        list_slot.reshape(128, 128),
        coarse,
        codebook,
    )
    return updated, nearest.reshape(ROWS)


def solution(mesh):
    placed = (P("rep", "feat"), P("rep"), P("rep"), P(), P("rep", None), P(("rep", "feat"), None))
    return jax.shard_map(
        per_device,
        mesh=mesh,
        in_specs=placed,
        out_specs=(P(("rep", "feat"), None), P("rep")),
        check_vma=False,
    )
```

```python
import jax
import jax.numpy as jnp
from jax import lax
from jax.experimental import pallas as pl
from jax.experimental.pallas import tpu as pltpu
from jax.sharding import PartitionSpec as P

NZ, NY, NX = 8, 4, 4
PLANE = NY * NX
CHIPS = NZ * PLANE
FEATURES = 768
HALF = FEATURES // 2
PART = FEATURES // 3
ROWS = 512
CAP = 8
CHUNK = PLANE * CAP
SLOTS = CHIPS * CAP
PRIOR = 8.0
MESH = pl.DeviceIdType.MESH
F32, BF16, I32 = jnp.float32, jnp.bfloat16, jnp.int32
SLAB = 4 * NZ
FAR_Z = (4, 3, 5, 2, 6, 1, 7)
FAR_P = (10, 6, 9, 11, 14, 2, 5, 7, 8, 13, 15, 1, 3, 4, 12)
PARTS = 3


def iota(shape, axis):
    return lax.broadcasted_iota(I32, shape, axis)


def one_hot(mask):
    return jnp.where(mask, 1.0, 0.0).astype(BF16)


def dot(a, b, over=((1,), (0,))):
    return lax.dot_general(a, b, (over, ((), ())), preferred_element_type=F32)


def kernel(
    rows_hbm, lid_hbm, code_hbm, table_hbm, coarse_hbm, codebook_hbm,
    updated_ref, nearest_ref,
    rows_ref, lid_ref, code_ref, table_ref, coarse_ref, codebook_ref,
    send_a, mid_a, recv_a, send_b, mid_b, recv_b,
    tag_send, tag_mid, tag_recv, pick_b, base_ref, res_full, row_rhs, acc_ref,
    sums_own, sums_sib, books, near_own, near_sib,
    load_sem, z_send, z_recv, p_send, p_recv, tag_sem, swap_send, swap_recv, g_send, g_recv, r_send, r_recv,
):
    rep, feat = lax.axis_index("rep"), lax.axis_index("feat")
    z, y, x = rep >> 4, (rep >> 2) & 3, rep & 3

    def chip(dz, dy, dx):
        at = (((z + dz) & (NZ - 1)) << 4) | (((y + dy) & 3) << 2) | ((x + dx) & 3)
        return (at, feat)

    def in_plane(p, sign=1):
        return chip(0, sign * (p >> 2), sign * (p & 3))

    sibling = (rep, 1 - feat)

    def remote(src, dst, send_sem, recv_sem, to):
        return pltpu.make_async_remote_copy(
            src_ref=src, dst_ref=dst, send_sem=send_sem, recv_sem=recv_sem,
            device_id=to, device_id_type=MESH,
        )

    def wait_bytes(ref, sem):
        pltpu.make_async_copy(ref, ref, sem).wait()

    loads = [
        pltpu.make_async_copy(src, dst, load_sem.at[i])
        for i, (src, dst) in enumerate(
            (
                (lid_hbm, lid_ref),
                (table_hbm, table_ref),
                (code_hbm, code_ref),
                (rows_hbm, rows_ref),
                (coarse_hbm.at[:, pl.ds(pl.multiple_of(feat * HALF, 128), HALF)], coarse_ref),
                (codebook_hbm, codebook_ref),
            )
        )
    ]
    for load in loads:
        load.start()
    barrier = pltpu.get_barrier_semaphore()
    far = [chip(dz, 0, 0) for dz in FAR_Z] + [in_plane(p) for p in FAR_P]
    for i in range(PLANE + NZ - 2):
        pl.semaphore_signal(barrier, inc=1, device_id=far[i // 2 + (i % 2) * 7 if i < 14 else i], device_id_type=MESH)
    pl.semaphore_signal(barrier, inc=1, device_id=sibling, device_id_type=MESH)

    for load in loads[:3]:
        load.wait()
    lid, code, table = lid_ref[...], code_ref[...], table_ref[...]
    high = one_hot(iota((128, ROWS), 0) == (lid >> 7))
    low = iota((128, ROWS), 0) == (lid & 127)

    def look_up(t):
        got = dot(t.astype(F32).astype(BF16), high, ((0,), (0,)))
        return jnp.sum(jnp.where(low, got, 0.0), axis=0, keepdims=True)

    owner, local = look_up(table >> 7), look_up(table & 127)

    def offset(chip_id):
        return (
            (((chip_id >> 4) - z) & (NZ - 1)) * PLANE
            + (((chip_id >> 2) - y) & (NY - 1)) * NX
            + ((chip_id - x) & (NX - 1))
        )

    def lines(values, width):
        line, out = iota((16, width), 0), jnp.zeros((16, width), F32)
        for i, v in enumerate(values):
            out = jnp.where(line == i, v, out)
        return out.astype(BF16)

    owner_col = dot(lines([owner], ROWS), lines([1.0], ROWS), ((0,), (0,)))
    same = (owner_col == owner) & (iota((ROWS, ROWS), 0) < iota((ROWS, ROWS), 1))
    rank = jnp.sum(jnp.where(same, 1.0, 0.0), axis=0, keepdims=True).astype(I32)
    dest = offset(owner.astype(I32)) * CAP + rank
    tags = lines([local, (code >> 6).astype(F32), (code & 63).astype(F32), 1.0], ROWS)
    loads[3].wait()

    def pack_rows(c, carry):
        pick = one_hot(iota((CHUNK, ROWS), 0) + c * CHUNK == dest)
        out = dot(pick, rows_ref[...])
        for i in range(PARTS):
            send_a[i, c] = out[:, i * 128 : (i + 1) * 128].reshape(PLANE, CAP, 128).astype(BF16)
        t = dot(tags, pick, ((1,), (1,)))
        tag_send[0, c] = t[0:1] * 4096.0 + t[1:2] * 64.0 + t[2:3] + t[3:4]
        return carry

    lax.fori_loop(0, NZ, pack_rows, 0)
    loads[4].wait()
    loads[5].wait()
    pl.semaphore_wait(barrier, PLANE + NZ - 1)

    def tags_along_z(n, sign):
        for dz in FAR_Z:
            remote(tag_send.at[n, dz], tag_mid.at[n, dz], tag_sem.at[n, 0], tag_sem.at[n, 1],
                   chip(sign * dz, 0, 0)).start()
        tag_mid[n, 0] = tag_send[n, 0]

    def tags_in_plane(n, sign):
        wait_bytes(tag_mid.at[n, pl.ds(1, NZ - 1)], tag_sem.at[n, 1])
        for p in FAR_P:
            remote(tag_mid.at[n], tag_recv.at[n, p], tag_sem.at[n, 2], tag_sem.at[n, 3],
                   in_plane(p, sign)).start()
        tag_recv[n, 0] = tag_mid[n]

    def tags_got(n):
        wait_bytes(tag_recv.at[n, pl.ds(1, PLANE - 1)], tag_sem.at[n, 3])
        lane = iota((NZ, 128), 1) >> 3
        out = jnp.zeros((NZ, 128), F32)
        for p in range(PLANE):
            out = jnp.where(lane == p, tag_recv[n, p].reshape(NZ, 128), out)
        return out

    def tags_sent(n):
        wait_bytes(tag_send.at[n, pl.ds(1, NZ - 1)], tag_sem.at[n, 0])
        wait_bytes(tag_recv.at[n, pl.ds(1, PLANE - 1)], tag_sem.at[n, 2])

    def in_a_row(t):
        return jnp.concatenate([t[c : c + 1] for c in range(NZ)], axis=1)

    def along_z(n, src, mid, i):
        for dz in FAR_Z:
            remote(src.at[i, dz], mid.at[i, dz], z_send.at[n], z_recv.at[n, i], chip(dz, 0, 0)).start()
        mid[i, 0] = src[i, 0]

    def forward(n, mid, dst, i):
        wait_bytes(mid.at[i, pl.ds(1, NZ - 1)], z_recv.at[n, i])
        for p in FAR_P:
            remote(mid.at[i, :, p], dst.at[i, :, p], p_send.at[n], p_recv.at[n, i], in_plane(p)).start()
        dst[i, :, 0] = mid[i, :, 0]

    def arrived(n, dst, i):
        wait_bytes(dst.at[i, :, pl.ds(1, PLANE - 1)], p_recv.at[n, i])
        return dst[i].astype(F32).reshape(SLOTS, 128)

    def all_sent(n, src, dst):
        for i in range(PARTS):
            wait_bytes(src.at[i, pl.ds(1, NZ - 1)], z_send.at[n])
            wait_bytes(dst.at[i, :, pl.ds(1, PLANE - 1)], p_send.at[n])

    tags_along_z(0, 1)
    for i in range(PARTS):
        along_z(0, send_a, mid_a, i)
    tags_in_plane(0, 1)
    forward(0, mid_a, recv_a, 0)

    got = in_a_row(tags_got(0)).astype(I32) - 1
    local_b = got >> 12
    code_b = jnp.where(got >= 0, got & 4095, -1)
    half_b = ((z - (iota((1, SLOTS), 1) >> 7)) & (NZ - 1)) >> 2
    key = jnp.where(got >= 0, (code_b >> 4) * 2 + half_b, -1)
    key_f = key.astype(F32)
    key_lines = lines([(key >> 4).astype(F32), (key & 15).astype(F32)], SLOTS)
    weights = lines([16.0, 1.0], SLOTS)
    rank_b = jnp.zeros((1, SLOTS), F32)
    for c in range(NZ):
        key_col = dot(key_lines[:, c * CHUNK : (c + 1) * CHUNK], weights, ((0,), (0,)))
        before = iota((CHUNK, SLOTS), 0) + c * CHUNK < iota((CHUNK, SLOTS), 1)
        hit = jnp.where((key_col == key_f) & before, 1.0, 0.0)
        rank_b += jnp.sum(hit, axis=0, keepdims=True)
    dest_b = offset(code_b >> 5) * CAP + ((code_b >> 4) & 1) * 4 + half_b * 2 + rank_b.astype(I32)
    dest_b = jnp.where(got >= 0, dest_b, -1)
    tags_b = lines([(code_b & 31).astype(F32), 1.0], SLOTS)

    def plan(c, carry):
        pick = one_hot(iota((CHUNK, SLOTS), 0) + c * CHUNK == dest_b)
        pick_b[pl.ds(c * CHUNK, CHUNK), :] = pick
        t = dot(tags_b, pick, ((1,), (1,)))
        tag_send[1, c] = t[0:1] + t[1:2]
        return carry

    lax.fori_loop(0, NZ, plan, 0)
    tags_along_z(1, 1)
    for c in range(NZ):
        pick = one_hot(iota((128, CHUNK), 0) == local_b[:, c * CHUNK : (c + 1) * CHUNK])
        base = dot(pick, coarse_ref[...], ((0,), (0,)))
        base_ref[c * CHUNK : (c + 1) * CHUNK, :] = base.astype(BF16)

    def residual(i):
        at = slice(i * 128, (i + 1) * 128)
        res = (arrived(0, recv_a, i) - base_ref[:, at].astype(F32)).astype(BF16)
        res_full[feat, :, at] = res
        send_b[i] = dot(pick_b[...], res).reshape(NZ, PLANE, CAP, 128).astype(BF16)
        along_z(1, send_b, mid_b, i)

    forward(0, mid_a, recv_a, 1)
    residual(0)
    forward(0, mid_a, recv_a, 2)
    tags_in_plane(1, 1)
    residual(1)
    residual(2)
    swap_res = remote(res_full.at[feat], res_full.at[feat], swap_send.at[0], swap_recv.at[0], sibling)
    swap_res.start()
    forward(1, mid_b, recv_b, 0)

    word = in_a_row(tags_got(1)).astype(I32) - 1
    named = iota((32, SLOTS), 0) == word
    counts = jnp.sum(jnp.where(named, 1.0, 0.0), axis=1, keepdims=True)
    count = jnp.where(feat == 0, counts[:16], counts[16:])
    named = one_hot(named)

    def rows_side():
        swap_res.wait()
        ones = jnp.ones((16, HALF), BF16)
        norm = jnp.zeros((16, SLOTS), F32)
        for f in range(2):
            r = res_full[f].astype(F32)
            for i in range(PARTS):
                at = i * 2 + f
                row_rhs[:, at * 128 : (at + 1) * 128] = (-2.0 * r[:, i * 128 : (i + 1) * 128]).astype(BF16)
            sq = r * r
            sq_hi = sq.astype(BF16)
            sq_lo = (sq - sq_hi.astype(F32)).astype(BF16)
            norm += dot(ones, sq_hi, ((1,), (1,))) + dot(ones, sq_lo, ((1,), (1,)))
        return norm[0:1]

    row_norm = rows_side()

    def order(b):
        first, last = ((x, y), (y, x))[b % 2]
        line = (last * 4 + first) * NZ
        return line + z, line, last

    def on(axis, i):
        return chip(0, i, 0) if axis == 0 else chip(0, 0, i)

    def gather_z(b, block):
        at, _, _ = order(b)
        books[b, at] = block
        ref = books.at[b, at]
        for dz in FAR_Z:
            remote(ref, ref, g_send.at[b, 0], g_recv.at[b, 0], chip(dz, 0, 0)).start()

    def some(b, n):
        return books.at[b, pl.ds(0, n)]

    def gather_line(b):
        wait_bytes(some(b, NZ - 1), g_recv.at[b, 0])
        _, line, _ = order(b)
        ref = books.at[b, pl.ds(line, NZ)]
        for i in (2, 1, 3):
            remote(ref, ref, g_send.at[b, 1], g_recv.at[b, 1], on(1 - b % 2, i)).start()

    def ring(b, k):
        _, _, last = order(b)
        for d, i in enumerate((1, 3)):
            if k == 0:
                ref = books.at[b, pl.ds(last * SLAB, SLAB)]
            else:
                ref = books.at[b, pl.ds(((last - i) & 3) * SLAB + d * (SLAB // 2), SLAB // 2)]
            remote(ref, ref, r_send.at[b, k, d], r_recv.at[b, k, d], on(b % 2, i)).start()

    def gather_ring(b):
        wait_bytes(some(b, 3 * NZ), g_recv.at[b, 1])
        ring(b, 0)

    def slab_direct(b):
        wait_bytes(some(b, 3 * NZ), g_recv.at[b, 1])
        _, _, last = order(b)
        ref = books.at[b, pl.ds(last * SLAB, SLAB)]
        for i in (2, 1, 3):
            remote(ref, ref, r_send.at[b, 0, 0], r_recv.at[b, 0, 0], on(b % 2, i)).start()

    def ring_came(b, k):
        for d in range(2):
            wait_bytes(some(b, SLAB >> k), r_recv.at[b, k, d])

    def gather_on(b):
        ring_came(b, 0)
        ring(b, 1)

    def both(do, i):
        do(2 * i)
        do(2 * i + 1)

    def update(i):
        sums = dot(named, arrived(1, recv_b, i).astype(BF16))
        sums_own[i, 0], sums_own[i, 1] = sums[:16], sums[16:]
        swap = remote(sums_own.at[i, 1 - feat], sums_sib.at[i], swap_send.at[1 + i], swap_recv.at[1 + i], sibling)
        swap.start()
        mine = jnp.where(feat == 0, sums[:16], sums[16:])
        swap.wait()
        theirs = sums_sib[i]
        block = []
        for f in range(2):
            at = slice(f * HALF + i * 128, f * HALF + (i + 1) * 128)
            total = jnp.where(feat == f, mine, theirs)
            new = (total + PRIOR * codebook_ref[:, at]) / (count + PRIOR)
            updated_ref[:, at] = new
            block.append(new.astype(BF16))
        for f in range(2):
            gather_z(2 * i + f, block[f])

    forward(1, mid_b, recv_b, 1)
    update(0)
    forward(1, mid_b, recv_b, 2)
    both(gather_line, 0)
    update(1)
    both(gather_ring, 0)
    update(2)
    both(gather_line, 1)
    both(gather_on, 0)
    both(gather_ring, 1)
    both(gather_line, 2)
    both(gather_on, 1)
    both(slab_direct, 2)
    both(lambda b: ring_came(b, 1), 0)
    both(lambda b: ring_came(b, 1), 1)

    def blocks(b, c):
        at = [i if b % 2 == 0 else i % 4 * 4 + i // 4 for i in range(PLANE)]
        return jnp.concatenate([books[b, i * NZ + c] for i in at], axis=0)

    def products(c, pieces):
        piece = jnp.concatenate([blocks(b, c) for b in pieces], axis=1)
        f = piece.astype(F32)
        at = slice(pieces[0] * 128, (pieces[-1] + 1) * 128)
        return dot(piece, row_rhs[:, at], ((1,), (1,))) + jnp.sum(f * f, axis=1, keepdims=True)

    def begin(c, carry):
        acc_ref[c] = products(c, (0, 1, 2, 3))
        return carry

    lax.fori_loop(0, NZ, begin, 0)
    both(lambda b: wait_bytes(some(b, 3 * SLAB), r_recv.at[b, 0, 0]), 2)

    def book_sent():
        for b in range(2 * PARTS):
            wait_bytes(some(b, NZ - 1), g_send.at[b, 0])
            wait_bytes(some(b, 3 * NZ), g_send.at[b, 1])
            if b >= 4:
                wait_bytes(some(b, 3 * SLAB), r_send.at[b, 0, 0])
                continue
            for k in range(2):
                for d in range(2):
                    wait_bytes(some(b, SLAB >> k), r_send.at[b, k, d])


    def finish(c, best):
        for i in range(2):
            dist = acc_ref[2 * c + i] + products(2 * c + i, (4, 5))
            best = jnp.minimum(best, jnp.min(dist.reshape(32, 8, SLOTS), axis=0))
        return best

    best = lax.fori_loop(0, NZ // 2, finish, jnp.full((8, SLOTS), 3e38, F32))
    best = (jnp.min(best, axis=0, keepdims=True) + row_norm) / FEATURES
    for c in range(NZ):
        tag_send[2, c] = best[:, c * CHUNK : (c + 1) * CHUNK]

    tags_along_z(2, -1)
    tags_in_plane(2, -1)
    back = tags_got(2)
    parts = []
    for _ in range(3):
        parts.append(back.astype(BF16).astype(F32))
        back = back - parts[-1]
    lane = one_hot(iota((128, ROWS), 0) == (dest & 127))
    near = dot(jnp.concatenate(parts, axis=0).astype(BF16), lane)
    near = near[:8] + near[8:16] + near[16:]
    near = jnp.sum(jnp.where(iota((NZ, ROWS), 0) == (dest >> 7), near, 0.0), axis=0, keepdims=True)
    near_own[...] = near
    swap_near = remote(near_own, near_sib, swap_send.at[4], swap_recv.at[4], sibling)
    swap_near.start()

    for n in range(3):
        tags_sent(n)
    all_sent(0, send_a, recv_a)
    all_sent(1, send_b, recv_b)
    book_sent()
    swap_near.wait()
    nearest_ref[...] = jnp.minimum(near, near_sib[...])


def per_device(rows, list_ids, code_ids, list_slot, coarse, codebook):
    vmem, hbm = pl.BlockSpec(memory_space=pltpu.VMEM), pl.BlockSpec(memory_space=pl.ANY)
    messages = pltpu.VMEM((PARTS, NZ, PLANE, CAP, 128), BF16)
    dma = pltpu.SemaphoreType.DMA
    updated, nearest = pl.pallas_call(
        kernel,
        out_shape=(
            jax.ShapeDtypeStruct((16, FEATURES), F32),
            jax.ShapeDtypeStruct((1, ROWS), F32),
        ),
        in_specs=[hbm] * 6,
        out_specs=(vmem, vmem),
        scratch_shapes=[
            pltpu.VMEM((ROWS, HALF), BF16),
            pltpu.VMEM((1, ROWS), I32),
            pltpu.VMEM((1, ROWS), I32),
            pltpu.VMEM((128, 128), I32),
            pltpu.VMEM((128, HALF), BF16),
            pltpu.VMEM((16, FEATURES), F32),
            messages, messages, messages, messages, messages, messages,
            pltpu.VMEM((3, NZ, 1, 128), F32),
            pltpu.VMEM((3, NZ, 1, 128), F32),
            pltpu.VMEM((3, PLANE, NZ, 1, 128), F32),
            pltpu.VMEM((SLOTS, SLOTS), BF16),
            pltpu.VMEM((SLOTS, HALF), BF16),
            pltpu.VMEM((2, SLOTS, HALF), BF16),
            pltpu.VMEM((SLOTS, FEATURES), BF16),
            pltpu.VMEM((NZ, 256, SLOTS), F32),
            pltpu.VMEM((PARTS, 2, 16, 128), F32),
            pltpu.VMEM((PARTS, 16, 128), F32),
            pltpu.VMEM((2 * PARTS, CHIPS, 16, 128), BF16),
            pltpu.VMEM((1, ROWS), F32),
            pltpu.VMEM((1, ROWS), F32),
            dma((6,)), dma((2,)), dma((2, PARTS)), dma((2,)), dma((2, PARTS)), dma((3, 4)), dma((5,)), dma((5,)),
            dma((6, 2)), dma((6, 2)), dma((6, 2, 2)), dma((6, 2, 2)),
        ],
        compiler_params=pltpu.CompilerParams(
            collective_id=0, has_side_effects=True, vmem_limit_bytes=63 * 2**20
        ),
    )(
        rows,
        list_ids.reshape(1, ROWS),
        code_ids.reshape(1, ROWS),
        list_slot.reshape(128, 128),
        coarse,
        codebook,
    )
    return updated, nearest.reshape(ROWS)


def solution(mesh):
    placed = (P("rep", "feat"), P("rep"), P("rep"), P(), P("rep", None), P(("rep", "feat"), None))
    return jax.shard_map(
        per_device,
        mesh=mesh,
        in_specs=placed,
        out_specs=(P(("rep", "feat"), None), P("rep")),
        check_vma=False,
    )
```

```python
import jax
import jax.numpy as jnp
from jax import lax
from jax.experimental import pallas as pl
from jax.experimental.pallas import tpu as pltpu
from jax.sharding import PartitionSpec as P

NZ, NY, NX = 8, 4, 4
PLANE = NY * NX
CHIPS = NZ * PLANE
FEATURES = 768
HALF = FEATURES // 2
PART = FEATURES // 3
ROWS = 512
CAP = 8
CHUNK = PLANE * CAP
SLOTS = CHIPS * CAP
PRIOR = 8.0
MESH = pl.DeviceIdType.MESH
F32, BF16, I32 = jnp.float32, jnp.bfloat16, jnp.int32
SLAB = 4 * NZ
FAR_Z = (4, 3, 5, 2, 6, 1, 7)
FAR_P = (10, 6, 9, 11, 14, 2, 5, 7, 8, 13, 15, 1, 3, 4, 12)
PARTS = 3


def iota(shape, axis):
    return lax.broadcasted_iota(I32, shape, axis)


def one_hot(mask):
    return jnp.where(mask, 1.0, 0.0).astype(BF16)


def dot(a, b, over=((1,), (0,))):
    return lax.dot_general(a, b, (over, ((), ())), preferred_element_type=F32)


def kernel(
    rows_hbm, lid_hbm, code_hbm, table_hbm, coarse_hbm, codebook_hbm,
    updated_ref, nearest_ref,
    rows_ref, lid_ref, code_ref, table_ref, coarse_ref, codebook_ref,
    send_a, mid_a, recv_a, send_b, mid_b, recv_b,
    tag_send, tag_mid, tag_recv, pick_b, base_ref, res_full, row_rhs, acc_ref,
    sums_own, sums_sib, books, near_own, near_sib,
    load_sem, z_send, z_recv, p_send, p_recv, tag_sem, swap_send, swap_recv, g_send, g_recv, r_send, r_recv,
):
    rep, feat = lax.axis_index("rep"), lax.axis_index("feat")
    z, y, x = rep >> 4, (rep >> 2) & 3, rep & 3

    def chip(dz, dy, dx):
        at = (((z + dz) & (NZ - 1)) << 4) | (((y + dy) & 3) << 2) | ((x + dx) & 3)
        return (at, feat)

    def in_plane(p, sign=1):
        return chip(0, sign * (p >> 2), sign * (p & 3))

    sibling = (rep, 1 - feat)

    def remote(src, dst, send_sem, recv_sem, to):
        return pltpu.make_async_remote_copy(
            src_ref=src, dst_ref=dst, send_sem=send_sem, recv_sem=recv_sem,
            device_id=to, device_id_type=MESH,
        )

    def wait_bytes(ref, sem):
        pltpu.make_async_copy(ref, ref, sem).wait()

    loads = [
        pltpu.make_async_copy(src, dst, load_sem.at[i])
        for i, (src, dst) in enumerate(
            (
                (lid_hbm, lid_ref),
                (table_hbm, table_ref),
                (code_hbm, code_ref),
                (rows_hbm, rows_ref),
                (coarse_hbm.at[:, pl.ds(pl.multiple_of(feat * HALF, 128), HALF)], coarse_ref),
                (codebook_hbm, codebook_ref),
            )
        )
    ]
    for load in loads:
        load.start()
    barrier = pltpu.get_barrier_semaphore()
    far = [chip(dz, 0, 0) for dz in FAR_Z] + [in_plane(p) for p in FAR_P]
    for i in range(PLANE + NZ - 2):
        pl.semaphore_signal(barrier, inc=1, device_id=far[i // 2 + (i % 2) * 7 if i < 14 else i], device_id_type=MESH)
    pl.semaphore_signal(barrier, inc=1, device_id=sibling, device_id_type=MESH)

    for load in loads[:3]:
        load.wait()
    lid, code, table = lid_ref[...], code_ref[...], table_ref[...]
    high = one_hot(iota((128, ROWS), 0) == (lid >> 7))
    low = iota((128, ROWS), 0) == (lid & 127)

    def look_up(t):
        got = dot(t.astype(F32).astype(BF16), high, ((0,), (0,)))
        return jnp.sum(jnp.where(low, got, 0.0), axis=0, keepdims=True)

    owner, local = look_up(table >> 7), look_up(table & 127)

    def offset(chip_id):
        return (
            (((chip_id >> 4) - z) & (NZ - 1)) * PLANE
            + (((chip_id >> 2) - y) & (NY - 1)) * NX
            + ((chip_id - x) & (NX - 1))
        )

    def lines(values, width):
        line, out = iota((16, width), 0), jnp.zeros((16, width), F32)
        for i, v in enumerate(values):
            out = jnp.where(line == i, v, out)
        return out.astype(BF16)

    owner_col = dot(lines([owner], ROWS), lines([1.0], ROWS), ((0,), (0,)))
    same = (owner_col == owner) & (iota((ROWS, ROWS), 0) < iota((ROWS, ROWS), 1))
    rank = jnp.sum(jnp.where(same, 1.0, 0.0), axis=0, keepdims=True).astype(I32)
    dest = offset(owner.astype(I32)) * CAP + rank
    tags = lines([local, (code >> 6).astype(F32), (code & 63).astype(F32), 1.0], ROWS)
    loads[3].wait()

    def pack_rows(c, carry):
        pick = one_hot(iota((CHUNK, ROWS), 0) + c * CHUNK == dest)
        out = dot(pick, rows_ref[...])
        for i in range(PARTS):
            send_a[i, c] = out[:, i * 128 : (i + 1) * 128].reshape(PLANE, CAP, 128).astype(BF16)
        t = dot(tags, pick, ((1,), (1,)))
        tag_send[0, c] = t[0:1] * 4096.0 + t[1:2] * 64.0 + t[2:3] + t[3:4]
        return carry

    lax.fori_loop(0, NZ, pack_rows, 0)
    loads[4].wait()
    loads[5].wait()
    pl.semaphore_wait(barrier, PLANE + NZ - 1)

    def tags_along_z(n, sign):
        for dz in FAR_Z:
            remote(tag_send.at[n, dz], tag_mid.at[n, dz], tag_sem.at[n, 0], tag_sem.at[n, 1],
                   chip(sign * dz, 0, 0)).start()
        tag_mid[n, 0] = tag_send[n, 0]

    def tags_in_plane(n, sign):
        wait_bytes(tag_mid.at[n, pl.ds(1, NZ - 1)], tag_sem.at[n, 1])
        for p in FAR_P:
            remote(tag_mid.at[n], tag_recv.at[n, p], tag_sem.at[n, 2], tag_sem.at[n, 3],
                   in_plane(p, sign)).start()
        tag_recv[n, 0] = tag_mid[n]

    def tags_got(n):
        wait_bytes(tag_recv.at[n, pl.ds(1, PLANE - 1)], tag_sem.at[n, 3])
        lane = iota((NZ, 128), 1) >> 3
        out = jnp.zeros((NZ, 128), F32)
        for p in range(PLANE):
            out = jnp.where(lane == p, tag_recv[n, p].reshape(NZ, 128), out)
        return out

    def tags_sent(n):
        wait_bytes(tag_send.at[n, pl.ds(1, NZ - 1)], tag_sem.at[n, 0])
        wait_bytes(tag_recv.at[n, pl.ds(1, PLANE - 1)], tag_sem.at[n, 2])

    def in_a_row(t):
        return jnp.concatenate([t[c : c + 1] for c in range(NZ)], axis=1)

    def along_z(n, src, mid, i):
        for dz in FAR_Z:
            remote(src.at[i, dz], mid.at[i, dz], z_send.at[n], z_recv.at[n, i], chip(dz, 0, 0)).start()
        mid[i, 0] = src[i, 0]

    def forward(n, mid, dst, i):
        wait_bytes(mid.at[i, pl.ds(1, NZ - 1)], z_recv.at[n, i])
        for p in FAR_P:
            remote(mid.at[i, :, p], dst.at[i, :, p], p_send.at[n], p_recv.at[n, i], in_plane(p)).start()
        dst[i, :, 0] = mid[i, :, 0]

    def arrived(n, dst, i):
        wait_bytes(dst.at[i, :, pl.ds(1, PLANE - 1)], p_recv.at[n, i])
        return dst[i].astype(F32).reshape(SLOTS, 128)

    def all_sent(n, src, dst):
        for i in range(PARTS):
            wait_bytes(src.at[i, pl.ds(1, NZ - 1)], z_send.at[n])
            wait_bytes(dst.at[i, :, pl.ds(1, PLANE - 1)], p_send.at[n])

    tags_along_z(0, 1)
    for i in range(PARTS):
        along_z(0, send_a, mid_a, i)
    tags_in_plane(0, 1)
    forward(0, mid_a, recv_a, 0)

    got = in_a_row(tags_got(0)).astype(I32) - 1
    local_b = got >> 12
    code_b = jnp.where(got >= 0, got & 4095, -1)
    half_b = ((z - (iota((1, SLOTS), 1) >> 7)) & (NZ - 1)) >> 2
    key = jnp.where(got >= 0, (code_b >> 4) * 2 + half_b, -1)
    key_f = key.astype(F32)
    key_lines = lines([(key >> 4).astype(F32), (key & 15).astype(F32)], SLOTS)
    weights = lines([16.0, 1.0], SLOTS)
    rank_b = jnp.zeros((1, SLOTS), F32)
    for c in range(NZ):
        key_col = dot(key_lines[:, c * CHUNK : (c + 1) * CHUNK], weights, ((0,), (0,)))
        before = iota((CHUNK, SLOTS), 0) + c * CHUNK < iota((CHUNK, SLOTS), 1)
        hit = jnp.where((key_col == key_f) & before, 1.0, 0.0)
        rank_b += jnp.sum(hit, axis=0, keepdims=True)
    dest_b = offset(code_b >> 5) * CAP + ((code_b >> 4) & 1) * 4 + half_b * 2 + rank_b.astype(I32)
    dest_b = jnp.where(got >= 0, dest_b, -1)
    tags_b = lines([(code_b & 31).astype(F32), 1.0], SLOTS)

    def plan(c, carry):
        pick = one_hot(iota((CHUNK, SLOTS), 0) + c * CHUNK == dest_b)
        pick_b[pl.ds(c * CHUNK, CHUNK), :] = pick
        t = dot(tags_b, pick, ((1,), (1,)))
        tag_send[1, c] = t[0:1] + t[1:2]
        return carry

    lax.fori_loop(0, NZ, plan, 0)
    tags_along_z(1, 1)
    for c in range(NZ):
        pick = one_hot(iota((128, CHUNK), 0) == local_b[:, c * CHUNK : (c + 1) * CHUNK])
        base = dot(pick, coarse_ref[...], ((0,), (0,)))
        base_ref[c * CHUNK : (c + 1) * CHUNK, :] = base.astype(BF16)

    def residual(i):
        at = slice(i * 128, (i + 1) * 128)
        res = (arrived(0, recv_a, i) - base_ref[:, at].astype(F32)).astype(BF16)
        res_full[feat, :, at] = res
        send_b[i] = dot(pick_b[...], res).reshape(NZ, PLANE, CAP, 128).astype(BF16)
        along_z(1, send_b, mid_b, i)

    forward(0, mid_a, recv_a, 1)
    residual(0)
    forward(0, mid_a, recv_a, 2)
    tags_in_plane(1, 1)
    residual(1)
    residual(2)
    swap_res = remote(res_full.at[feat], res_full.at[feat], swap_send.at[0], swap_recv.at[0], sibling)
    swap_res.start()
    forward(1, mid_b, recv_b, 0)

    word = in_a_row(tags_got(1)).astype(I32) - 1
    named = iota((32, SLOTS), 0) == word
    counts = jnp.sum(jnp.where(named, 1.0, 0.0), axis=1, keepdims=True)
    count = jnp.where(feat == 0, counts[:16], counts[16:])
    named = one_hot(named)

    def rows_side():
        swap_res.wait()
        ones = jnp.ones((16, HALF), BF16)
        norm = jnp.zeros((16, SLOTS), F32)
        for f in range(2):
            r = res_full[f].astype(F32)
            for i in range(PARTS):
                at = i * 2 + f
                row_rhs[at * 128 : (at + 1) * 128, :] = (-2.0 * r[:, i * 128 : (i + 1) * 128]).T.astype(BF16)
            sq = r * r
            sq_hi = sq.astype(BF16)
            sq_lo = (sq - sq_hi.astype(F32)).astype(BF16)
            norm += dot(ones, sq_hi, ((1,), (1,))) + dot(ones, sq_lo, ((1,), (1,)))
        return norm[0:1]

    row_norm = rows_side()

    def order(b):
        first, last = ((x, y), (y, x))[b % 2]
        line = (last * 4 + first) * NZ
        return line + z, line, last

    def on(axis, i):
        return chip(0, i, 0) if axis == 0 else chip(0, 0, i)

    def gather_z(b, block):
        at, _, _ = order(b)
        books[b, at] = block
        ref = books.at[b, at]
        for dz in FAR_Z:
            remote(ref, ref, g_send.at[b, 0], g_recv.at[b, 0], chip(dz, 0, 0)).start()

    def some(b, n):
        return books.at[b, pl.ds(0, n)]

    def gather_line(b):
        wait_bytes(some(b, NZ - 1), g_recv.at[b, 0])
        _, line, _ = order(b)
        ref = books.at[b, pl.ds(line, NZ)]
        for i in (2, 1, 3):
            remote(ref, ref, g_send.at[b, 1], g_recv.at[b, 1], on(1 - b % 2, i)).start()

    def ring(b, k):
        _, _, last = order(b)
        for d, i in enumerate((1, 3)):
            if k == 0:
                ref = books.at[b, pl.ds(last * SLAB, SLAB)]
            else:
                ref = books.at[b, pl.ds(((last - i) & 3) * SLAB + d * (SLAB // 2), SLAB // 2)]
            remote(ref, ref, r_send.at[b, k, d], r_recv.at[b, k, d], on(b % 2, i)).start()

    def gather_ring(b):
        wait_bytes(some(b, 3 * NZ), g_recv.at[b, 1])
        ring(b, 0)

    def slab_direct(b):
        wait_bytes(some(b, 3 * NZ), g_recv.at[b, 1])
        _, _, last = order(b)
        ref = books.at[b, pl.ds(last * SLAB, SLAB)]
        for i in (2, 1, 3):
            remote(ref, ref, r_send.at[b, 0, 0], r_recv.at[b, 0, 0], on(b % 2, i)).start()

    def ring_came(b, k):
        for d in range(2):
            wait_bytes(some(b, SLAB >> k), r_recv.at[b, k, d])

    def gather_on(b):
        ring_came(b, 0)
        ring(b, 1)

    def both(do, i):
        do(2 * i)
        do(2 * i + 1)

    def update(i):
        sums = dot(named, arrived(1, recv_b, i).astype(BF16))
        sums_own[i, 0], sums_own[i, 1] = sums[:16], sums[16:]
        swap = remote(sums_own.at[i, 1 - feat], sums_sib.at[i], swap_send.at[1 + i], swap_recv.at[1 + i], sibling)
        swap.start()
        mine = jnp.where(feat == 0, sums[:16], sums[16:])
        swap.wait()
        theirs = sums_sib[i]
        block = []
        for f in range(2):
            at = slice(f * HALF + i * 128, f * HALF + (i + 1) * 128)
            total = jnp.where(feat == f, mine, theirs)
            new = (total + PRIOR * codebook_ref[:, at]) / (count + PRIOR)
            updated_ref[:, at] = new
            block.append(new.astype(BF16))
        for f in range(2):
            gather_z(2 * i + f, block[f])

    forward(1, mid_b, recv_b, 1)
    update(0)
    forward(1, mid_b, recv_b, 2)
    both(gather_line, 0)
    update(1)
    both(gather_ring, 0)
    update(2)
    both(gather_line, 1)
    both(gather_on, 0)
    both(gather_ring, 1)
    both(gather_line, 2)
    both(gather_on, 1)
    both(slab_direct, 2)
    both(lambda b: ring_came(b, 1), 0)
    both(lambda b: ring_came(b, 1), 1)

    def blocks(b, c):
        at = [i if b % 2 == 0 else i % 4 * 4 + i // 4 for i in range(PLANE)]
        return jnp.concatenate([books[b, i * NZ + c] for i in at], axis=0)

    def products(c, pieces):
        piece = jnp.concatenate(
            [jnp.concatenate([blocks(b, 2 * c + i) for b in pieces], axis=1) for i in range(2)], axis=0
        )
        f = piece.astype(F32)
        at = slice(pieces[0] * 128, (pieces[-1] + 1) * 128)
        return dot(piece, row_rhs[at, :]) + jnp.sum(f * f, axis=1, keepdims=True)

    def begin(c, carry):
        acc_ref[c] = products(c, (0, 1, 2, 3))
        return carry

    lax.fori_loop(0, NZ // 2, begin, 0)
    both(lambda b: wait_bytes(some(b, 3 * SLAB), r_recv.at[b, 0, 0]), 2)

    def book_sent():
        for b in range(2 * PARTS):
            wait_bytes(some(b, NZ - 1), g_send.at[b, 0])
            wait_bytes(some(b, 3 * NZ), g_send.at[b, 1])
            if b >= 4:
                wait_bytes(some(b, 3 * SLAB), r_send.at[b, 0, 0])
                continue
            for k in range(2):
                for d in range(2):
                    wait_bytes(some(b, SLAB >> k), r_send.at[b, k, d])


    def finish(c, best):
        dist = acc_ref[c] + products(c, (4, 5))
        return jnp.minimum(best, jnp.min(dist.reshape(64, 8, SLOTS), axis=0))

    best = lax.fori_loop(0, NZ // 2, finish, jnp.full((8, SLOTS), 3e38, F32))
    best = (jnp.min(best, axis=0, keepdims=True) + row_norm) / FEATURES
    for c in range(NZ):
        tag_send[2, c] = best[:, c * CHUNK : (c + 1) * CHUNK]

    tags_along_z(2, -1)
    tags_in_plane(2, -1)
    back = tags_got(2)
    parts = []
    for _ in range(3):
        parts.append(back.astype(BF16).astype(F32))
        back = back - parts[-1]
    lane = one_hot(iota((128, ROWS), 0) == (dest & 127))
    near = dot(jnp.concatenate(parts, axis=0).astype(BF16), lane)
    near = near[:8] + near[8:16] + near[16:]
    near = jnp.sum(jnp.where(iota((NZ, ROWS), 0) == (dest >> 7), near, 0.0), axis=0, keepdims=True)
    near_own[...] = near
    swap_near = remote(near_own, near_sib, swap_send.at[4], swap_recv.at[4], sibling)
    swap_near.start()

    for n in range(3):
        tags_sent(n)
    all_sent(0, send_a, recv_a)
    all_sent(1, send_b, recv_b)
    book_sent()
    swap_near.wait()
    nearest_ref[...] = jnp.minimum(near, near_sib[...])


def per_device(rows, list_ids, code_ids, list_slot, coarse, codebook):
    vmem, hbm = pl.BlockSpec(memory_space=pltpu.VMEM), pl.BlockSpec(memory_space=pl.ANY)
    messages = pltpu.VMEM((PARTS, NZ, PLANE, CAP, 128), BF16)
    dma = pltpu.SemaphoreType.DMA
    updated, nearest = pl.pallas_call(
        kernel,
        out_shape=(
            jax.ShapeDtypeStruct((16, FEATURES), F32),
            jax.ShapeDtypeStruct((1, ROWS), F32),
        ),
        in_specs=[hbm] * 6,
        out_specs=(vmem, vmem),
        scratch_shapes=[
            pltpu.VMEM((ROWS, HALF), BF16),
            pltpu.VMEM((1, ROWS), I32),
            pltpu.VMEM((1, ROWS), I32),
            pltpu.VMEM((128, 128), I32),
            pltpu.VMEM((128, HALF), BF16),
            pltpu.VMEM((16, FEATURES), F32),
            messages, messages, messages, messages, messages, messages,
            pltpu.VMEM((3, NZ, 1, 128), F32),
            pltpu.VMEM((3, NZ, 1, 128), F32),
            pltpu.VMEM((3, PLANE, NZ, 1, 128), F32),
            pltpu.VMEM((SLOTS, SLOTS), BF16),
            pltpu.VMEM((SLOTS, HALF), BF16),
            pltpu.VMEM((2, SLOTS, HALF), BF16),
            pltpu.VMEM((FEATURES, SLOTS), BF16),
            pltpu.VMEM((NZ // 2, 512, SLOTS), F32),
            pltpu.VMEM((PARTS, 2, 16, 128), F32),
            pltpu.VMEM((PARTS, 16, 128), F32),
            pltpu.VMEM((2 * PARTS, CHIPS, 16, 128), BF16),
            pltpu.VMEM((1, ROWS), F32),
            pltpu.VMEM((1, ROWS), F32),
            dma((6,)), dma((2,)), dma((2, PARTS)), dma((2,)), dma((2, PARTS)), dma((3, 4)), dma((5,)), dma((5,)),
            dma((6, 2)), dma((6, 2)), dma((6, 2, 2)), dma((6, 2, 2)),
        ],
        compiler_params=pltpu.CompilerParams(
            collective_id=0, has_side_effects=True, vmem_limit_bytes=63 * 2**20
        ),
    )(
        rows,
        list_ids.reshape(1, ROWS),
        code_ids.reshape(1, ROWS),
        list_slot.reshape(128, 128),
        coarse,
        codebook,
    )
    return updated, nearest.reshape(ROWS)


def solution(mesh):
    placed = (P("rep", "feat"), P("rep"), P("rep"), P(), P("rep", None), P(("rep", "feat"), None))
    return jax.shard_map(
        per_device,
        mesh=mesh,
        in_specs=placed,
        out_specs=(P(("rep", "feat"), None), P("rep")),
        check_vma=False,
    )
```

```python
import jax
import jax.numpy as jnp
from jax import lax
from jax.experimental import pallas as pl
from jax.experimental.pallas import tpu as pltpu
from jax.sharding import PartitionSpec as P

NZ, NY, NX = 8, 4, 4
PLANE = NY * NX
CHIPS = NZ * PLANE
FEATURES = 768
HALF = FEATURES // 2
PART = FEATURES // 3
ROWS = 512
CAP = 8
CHUNK = PLANE * CAP
SLOTS = CHIPS * CAP
PRIOR = 8.0
MESH = pl.DeviceIdType.MESH
F32, BF16, I32 = jnp.float32, jnp.bfloat16, jnp.int32
SLAB = 4 * NZ
FAR_Z = (4, 3, 5, 2, 6, 1, 7)
FAR_P = (10, 6, 9, 11, 14, 2, 5, 7, 8, 13, 15, 1, 3, 4, 12)
PARTS = 3


def iota(shape, axis):
    return lax.broadcasted_iota(I32, shape, axis)


def one_hot(mask):
    return jnp.where(mask, 1.0, 0.0).astype(BF16)


def dot(a, b, over=((1,), (0,))):
    return lax.dot_general(a, b, (over, ((), ())), preferred_element_type=F32)


def kernel(
    rows_hbm, lid_hbm, code_hbm, table_hbm, coarse_hbm, codebook_hbm,
    updated_ref, nearest_ref,
    rows_ref, lid_ref, code_ref, table_ref, coarse_ref, codebook_ref,
    send_a, mid_a, recv_a, send_b, mid_b, recv_b,
    tag_send, tag_mid, tag_recv, pick_b, base_ref, res_full, row_rhs, acc_ref,
    sums_own, sums_sib, books, min_mid,
    load_sem, z_send, z_recv, p_send, p_recv, tag_sem, swap_send, swap_recv, g_send, g_recv, r_send, r_recv,
):
    rep, feat = lax.axis_index("rep"), lax.axis_index("feat")
    z, y, x = rep >> 4, (rep >> 2) & 3, rep & 3

    def chip(dz, dy, dx):
        at = (((z + dz) & (NZ - 1)) << 4) | (((y + dy) & 3) << 2) | ((x + dx) & 3)
        return (at, feat)

    def in_plane(p, sign=1):
        return chip(0, sign * (p >> 2), sign * (p & 3))

    sibling = (rep, 1 - feat)

    def remote(src, dst, send_sem, recv_sem, to):
        return pltpu.make_async_remote_copy(
            src_ref=src, dst_ref=dst, send_sem=send_sem, recv_sem=recv_sem,
            device_id=to, device_id_type=MESH,
        )

    def wait_bytes(ref, sem):
        pltpu.make_async_copy(ref, ref, sem).wait()

    loads = [
        pltpu.make_async_copy(src, dst, load_sem.at[i])
        for i, (src, dst) in enumerate(
            (
                (lid_hbm, lid_ref),
                (table_hbm, table_ref),
                (code_hbm, code_ref),
                (rows_hbm, rows_ref),
                (coarse_hbm.at[:, pl.ds(pl.multiple_of(feat * HALF, 128), HALF)], coarse_ref),
                (codebook_hbm, codebook_ref),
            )
        )
    ]
    for load in loads:
        load.start()
    barrier = pltpu.get_barrier_semaphore()
    across = [(chip(dz, 0, 0)[0], 1 - feat) for dz in FAR_Z]
    far = [chip(dz, 0, 0) for dz in FAR_Z] + [in_plane(p) for p in FAR_P]
    far += across
    for i in range(PLANE + 2 * NZ - 3):
        pl.semaphore_signal(barrier, inc=1, device_id=far[i // 2 + (i % 2) * 7 if i < 14 else i], device_id_type=MESH)
    pl.semaphore_signal(barrier, inc=1, device_id=sibling, device_id_type=MESH)

    for load in loads[:3]:
        load.wait()
    lid, code, table = lid_ref[...], code_ref[...], table_ref[...]
    high = one_hot(iota((128, ROWS), 0) == (lid >> 7))
    low = iota((128, ROWS), 0) == (lid & 127)

    def look_up(t):
        got = dot(t.astype(F32).astype(BF16), high, ((0,), (0,)))
        return jnp.sum(jnp.where(low, got, 0.0), axis=0, keepdims=True)

    owner, local = look_up(table >> 7), look_up(table & 127)

    def offset(chip_id):
        return (
            (((chip_id >> 4) - z) & (NZ - 1)) * PLANE
            + (((chip_id >> 2) - y) & (NY - 1)) * NX
            + ((chip_id - x) & (NX - 1))
        )

    def lines(values, width):
        line, out = iota((16, width), 0), jnp.zeros((16, width), F32)
        for i, v in enumerate(values):
            out = jnp.where(line == i, v, out)
        return out.astype(BF16)

    owner_col = dot(lines([owner], ROWS), lines([1.0], ROWS), ((0,), (0,)))
    same = (owner_col == owner) & (iota((ROWS, ROWS), 0) < iota((ROWS, ROWS), 1))
    rank = jnp.sum(jnp.where(same, 1.0, 0.0), axis=0, keepdims=True).astype(I32)
    dest = offset(owner.astype(I32)) * CAP + rank
    tags = lines([local, (code >> 6).astype(F32), (code & 63).astype(F32), 1.0], ROWS)
    loads[3].wait()

    def pack_rows(c, carry):
        pick = one_hot(iota((CHUNK, ROWS), 0) + c * CHUNK == dest)
        out = dot(pick, rows_ref[...])
        for i in range(PARTS):
            send_a[i, c] = out[:, i * 128 : (i + 1) * 128].reshape(PLANE, CAP, 128).astype(BF16)
        t = dot(tags, pick, ((1,), (1,)))
        tag_send[0, c] = t[0:1] * 4096.0 + t[1:2] * 64.0 + t[2:3] + t[3:4]
        return carry

    lax.fori_loop(0, NZ, pack_rows, 0)
    loads[4].wait()
    loads[5].wait()
    pl.semaphore_wait(barrier, PLANE + 2 * NZ - 2)

    def tags_along_z(n, sign):
        for dz in FAR_Z:
            remote(tag_send.at[n, dz], tag_mid.at[n, dz], tag_sem.at[n, 0], tag_sem.at[n, 1],
                   chip(sign * dz, 0, 0)).start()
        tag_mid[n, 0] = tag_send[n, 0]

    def tags_in_plane(n, sign):
        wait_bytes(tag_mid.at[n, pl.ds(1, NZ - 1)], tag_sem.at[n, 1])
        for p in FAR_P:
            remote(tag_mid.at[n], tag_recv.at[n, p], tag_sem.at[n, 2], tag_sem.at[n, 3],
                   in_plane(p, sign)).start()
        tag_recv[n, 0] = tag_mid[n]

    def tags_got(n):
        wait_bytes(tag_recv.at[n, pl.ds(1, PLANE - 1)], tag_sem.at[n, 3])
        lane = iota((NZ, 128), 1) >> 3
        out = jnp.zeros((NZ, 128), F32)
        for p in range(PLANE):
            out = jnp.where(lane == p, tag_recv[n, p].reshape(NZ, 128), out)
        return out

    def tags_sent(n):
        wait_bytes(tag_send.at[n, pl.ds(1, NZ - 1)], tag_sem.at[n, 0])
        wait_bytes(tag_recv.at[n, pl.ds(1, PLANE - 1)], tag_sem.at[n, 2])

    def in_a_row(t):
        return jnp.concatenate([t[c : c + 1] for c in range(NZ)], axis=1)

    def along_z(n, src, mid, i):
        for dz in FAR_Z:
            remote(src.at[i, dz], mid.at[i, dz], z_send.at[n], z_recv.at[n, i], chip(dz, 0, 0)).start()
        mid[i, 0] = src[i, 0]

    def forward(n, mid, dst, i):
        wait_bytes(mid.at[i, pl.ds(1, NZ - 1)], z_recv.at[n, i])
        for p in FAR_P:
            remote(mid.at[i, :, p], dst.at[i, :, p], p_send.at[n], p_recv.at[n, i], in_plane(p)).start()
        dst[i, :, 0] = mid[i, :, 0]

    def arrived(n, dst, i):
        wait_bytes(dst.at[i, :, pl.ds(1, PLANE - 1)], p_recv.at[n, i])
        return dst[i].astype(F32).reshape(SLOTS, 128)

    def all_sent(n, src, dst):
        for i in range(PARTS):
            wait_bytes(src.at[i, pl.ds(1, NZ - 1)], z_send.at[n])
            wait_bytes(dst.at[i, :, pl.ds(1, PLANE - 1)], p_send.at[n])

    tags_along_z(0, 1)
    for i in range(PARTS):
        along_z(0, send_a, mid_a, i)
    tags_in_plane(0, 1)
    forward(0, mid_a, recv_a, 0)

    got = in_a_row(tags_got(0)).astype(I32) - 1
    local_b = got >> 12
    code_b = jnp.where(got >= 0, got & 4095, -1)
    half_b = ((z - (iota((1, SLOTS), 1) >> 7)) & (NZ - 1)) >> 2
    key = jnp.where(got >= 0, (code_b >> 4) * 2 + half_b, -1)
    key_f = key.astype(F32)
    key_lines = lines([(key >> 4).astype(F32), (key & 15).astype(F32)], SLOTS)
    weights = lines([16.0, 1.0], SLOTS)
    rank_b = jnp.zeros((1, SLOTS), F32)
    for c in range(NZ):
        key_col = dot(key_lines[:, c * CHUNK : (c + 1) * CHUNK], weights, ((0,), (0,)))
        before = iota((CHUNK, SLOTS), 0) + c * CHUNK < iota((CHUNK, SLOTS), 1)
        hit = jnp.where((key_col == key_f) & before, 1.0, 0.0)
        rank_b += jnp.sum(hit, axis=0, keepdims=True)
    dest_b = offset(code_b >> 5) * CAP + ((code_b >> 4) & 1) * 4 + half_b * 2 + rank_b.astype(I32)
    dest_b = jnp.where(got >= 0, dest_b, -1)
    tags_b = lines([(code_b & 31).astype(F32), 1.0], SLOTS)

    def plan(c, carry):
        pick = one_hot(iota((CHUNK, SLOTS), 0) + c * CHUNK == dest_b)
        pick_b[pl.ds(c * CHUNK, CHUNK), :] = pick
        t = dot(tags_b, pick, ((1,), (1,)))
        tag_send[1, c] = t[0:1] + t[1:2]
        return carry

    lax.fori_loop(0, NZ, plan, 0)
    tags_along_z(1, 1)
    for c in range(NZ):
        pick = one_hot(iota((128, CHUNK), 0) == local_b[:, c * CHUNK : (c + 1) * CHUNK])
        base = dot(pick, coarse_ref[...], ((0,), (0,)))
        base_ref[c * CHUNK : (c + 1) * CHUNK, :] = base.astype(BF16)

    def residual(i):
        at = slice(i * 128, (i + 1) * 128)
        res = (arrived(0, recv_a, i) - base_ref[:, at].astype(F32)).astype(BF16)
        res_full[feat, :, at] = res
        send_b[i] = dot(pick_b[...], res).reshape(NZ, PLANE, CAP, 128).astype(BF16)
        along_z(1, send_b, mid_b, i)

    forward(0, mid_a, recv_a, 1)
    residual(0)
    forward(0, mid_a, recv_a, 2)
    tags_in_plane(1, 1)
    residual(1)
    residual(2)
    swap_res = remote(res_full.at[feat], res_full.at[feat], swap_send.at[0], swap_recv.at[0], sibling)
    swap_res.start()
    forward(1, mid_b, recv_b, 0)

    word = in_a_row(tags_got(1)).astype(I32) - 1
    named = iota((32, SLOTS), 0) == word
    counts = jnp.sum(jnp.where(named, 1.0, 0.0), axis=1, keepdims=True)
    count = jnp.where(feat == 0, counts[:16], counts[16:])
    named = one_hot(named)

    def rows_side():
        swap_res.wait()
        ones = jnp.ones((16, HALF), BF16)
        norm = jnp.zeros((16, SLOTS), F32)
        for f in range(2):
            r = res_full[f].astype(F32)
            for i in range(PARTS):
                at = i * 2 + f
                row_rhs[at * 128 : (at + 1) * 128, :] = (-2.0 * r[:, i * 128 : (i + 1) * 128]).T.astype(BF16)
            sq = r * r
            sq_hi = sq.astype(BF16)
            sq_lo = (sq - sq_hi.astype(F32)).astype(BF16)
            norm += dot(ones, sq_hi, ((1,), (1,))) + dot(ones, sq_lo, ((1,), (1,)))
        return norm[0:1]

    row_norm = rows_side()

    def order(b):
        first, last = ((x, y), (y, x))[b % 2]
        line = (last * 4 + first) * NZ
        return line + z, line, last

    def on(axis, i):
        return chip(0, i, 0) if axis == 0 else chip(0, 0, i)

    def gather_z(b, block):
        at, _, _ = order(b)
        books[b, at] = block
        ref = books.at[b, at]
        for dz in FAR_Z:
            remote(ref, ref, g_send.at[b, 0], g_recv.at[b, 0], chip(dz, 0, 0)).start()

    def some(b, n):
        return books.at[b, pl.ds(0, n)]

    def gather_line(b):
        wait_bytes(some(b, NZ - 1), g_recv.at[b, 0])
        _, line, _ = order(b)
        ref = books.at[b, pl.ds(line, NZ)]
        for i in (2, 1, 3):
            remote(ref, ref, g_send.at[b, 1], g_recv.at[b, 1], on(1 - b % 2, i)).start()

    def ring(b, k):
        _, _, last = order(b)
        for d, i in enumerate((1, 3)):
            if k == 0:
                ref = books.at[b, pl.ds(last * SLAB, SLAB)]
            else:
                ref = books.at[b, pl.ds(((last - i) & 3) * SLAB + d * (SLAB // 2), SLAB // 2)]
            remote(ref, ref, r_send.at[b, k, d], r_recv.at[b, k, d], on(b % 2, i)).start()

    def gather_ring(b):
        wait_bytes(some(b, 3 * NZ), g_recv.at[b, 1])
        ring(b, 0)

    def slab_direct(b):
        wait_bytes(some(b, 3 * NZ), g_recv.at[b, 1])
        _, _, last = order(b)
        ref = books.at[b, pl.ds(last * SLAB, SLAB)]
        for i in (2, 1, 3):
            remote(ref, ref, r_send.at[b, 0, 0], r_recv.at[b, 0, 0], on(b % 2, i)).start()

    def ring_came(b, k):
        for d in range(2):
            wait_bytes(some(b, SLAB >> k), r_recv.at[b, k, d])

    def gather_on(b):
        ring_came(b, 0)
        ring(b, 1)

    def both(do, i):
        do(2 * i)
        do(2 * i + 1)

    def update(i):
        sums = dot(named, arrived(1, recv_b, i).astype(BF16))
        sums_own[i, 0], sums_own[i, 1] = sums[:16], sums[16:]
        swap = remote(sums_own.at[i, 1 - feat], sums_sib.at[i], swap_send.at[1 + i], swap_recv.at[1 + i], sibling)
        swap.start()
        mine = jnp.where(feat == 0, sums[:16], sums[16:])
        swap.wait()
        theirs = sums_sib[i]
        block = []
        for f in range(2):
            at = slice(f * HALF + i * 128, f * HALF + (i + 1) * 128)
            total = jnp.where(feat == f, mine, theirs)
            new = (total + PRIOR * codebook_ref[:, at]) / (count + PRIOR)
            updated_ref[:, at] = new
            block.append(new.astype(BF16))
        for f in range(2):
            gather_z(2 * i + f, block[f])

    forward(1, mid_b, recv_b, 1)
    update(0)
    forward(1, mid_b, recv_b, 2)
    both(gather_line, 0)
    update(1)
    both(gather_ring, 0)
    update(2)
    both(gather_line, 1)
    both(gather_on, 0)
    both(gather_ring, 1)
    both(gather_line, 2)
    both(gather_on, 1)
    both(slab_direct, 2)
    both(lambda b: ring_came(b, 1), 0)
    both(lambda b: ring_came(b, 1), 1)

    def blocks(b, c):
        at = [i if b % 2 == 0 else i % 4 * 4 + i // 4 for i in range(PLANE)]
        return jnp.concatenate([books[b, i * NZ + c] for i in at], axis=0)

    def products(c, pieces):
        piece = jnp.concatenate(
            [jnp.concatenate([blocks(b, 2 * c + i) for b in pieces], axis=1) for i in range(2)], axis=0
        )
        f = piece.astype(F32)
        at = slice(pieces[0] * 128, (pieces[-1] + 1) * 128)
        return dot(piece, row_rhs[at, :]) + jnp.sum(f * f, axis=1, keepdims=True)

    def begin(c, carry):
        acc_ref[c] = products(c, (0, 1, 2, 3))
        return carry

    lax.fori_loop(0, NZ // 2, begin, 0)
    both(lambda b: wait_bytes(some(b, 3 * SLAB), r_recv.at[b, 0, 0]), 2)

    def book_sent():
        for b in range(2 * PARTS):
            wait_bytes(some(b, NZ - 1), g_send.at[b, 0])
            wait_bytes(some(b, 3 * NZ), g_send.at[b, 1])
            if b >= 4:
                wait_bytes(some(b, 3 * SLAB), r_send.at[b, 0, 0])
                continue
            for k in range(2):
                for d in range(2):
                    wait_bytes(some(b, SLAB >> k), r_send.at[b, k, d])


    def finish(c, best):
        dist = acc_ref[c] + products(c, (4, 5))
        return jnp.minimum(best, jnp.min(dist.reshape(64, 8, SLOTS), axis=0))

    best = lax.fori_loop(0, NZ // 2, finish, jnp.full((8, SLOTS), 3e38, F32))
    best = (jnp.min(best, axis=0, keepdims=True) + row_norm) / FEATURES
    for c in range(NZ):
        tag_send[2, c] = best[:, c * CHUNK : (c + 1) * CHUNK]

    min_mid[feat, 0] = best[:, :CHUNK]
    for dz in FAR_Z:
        to = chip(-dz, 0, 0)
        remote(tag_send.at[2, dz], min_mid.at[feat, dz], tag_sem.at[2, 0], tag_sem.at[2, 1], to).start()
        remote(tag_send.at[2, dz], min_mid.at[feat, dz], swap_send.at[4], swap_recv.at[4], (to[0], 1 - feat)).start()
    remote(tag_send.at[2, 0], min_mid.at[feat, 0], swap_send.at[4], swap_recv.at[4], sibling).start()
    for n in range(2):
        tags_sent(n)
    all_sent(0, send_a, recv_a)
    all_sent(1, send_b, recv_b)
    book_sent()
    wait_bytes(min_mid.at[0, pl.ds(1, NZ - 1)], tag_sem.at[2, 1])
    wait_bytes(min_mid.at[0], swap_recv.at[4])
    tag_mid[2] = jnp.minimum(min_mid[0], min_mid[1])
    for p in FAR_P:
        remote(tag_mid.at[2], tag_recv.at[2, p], tag_sem.at[2, 2], tag_sem.at[2, 3], in_plane(p, -1)).start()
    tag_recv[2, 0] = tag_mid[2]
    back = tags_got(2)
    parts = []
    for _ in range(3):
        parts.append(back.astype(BF16).astype(F32))
        back = back - parts[-1]
    lane = one_hot(iota((128, ROWS), 0) == (dest & 127))
    near = dot(jnp.concatenate(parts, axis=0).astype(BF16), lane)
    near = near[:8] + near[8:16] + near[16:]
    near = jnp.sum(jnp.where(iota((NZ, ROWS), 0) == (dest >> 7), near, 0.0), axis=0, keepdims=True)
    nearest_ref[...] = near
    tags_sent(2)
    wait_bytes(min_mid.at[0], swap_send.at[4])


def per_device(rows, list_ids, code_ids, list_slot, coarse, codebook):
    vmem, hbm = pl.BlockSpec(memory_space=pltpu.VMEM), pl.BlockSpec(memory_space=pl.ANY)
    messages = pltpu.VMEM((PARTS, NZ, PLANE, CAP, 128), BF16)
    dma = pltpu.SemaphoreType.DMA
    updated, nearest = pl.pallas_call(
        kernel,
        out_shape=(
            jax.ShapeDtypeStruct((16, FEATURES), F32),
            jax.ShapeDtypeStruct((1, ROWS), F32),
        ),
        in_specs=[hbm] * 6,
        out_specs=(vmem, vmem),
        scratch_shapes=[
            pltpu.VMEM((ROWS, HALF), BF16),
            pltpu.VMEM((1, ROWS), I32),
            pltpu.VMEM((1, ROWS), I32),
            pltpu.VMEM((128, 128), I32),
            pltpu.VMEM((128, HALF), BF16),
            pltpu.VMEM((16, FEATURES), F32),
            messages, messages, messages, messages, messages, messages,
            pltpu.VMEM((3, NZ, 1, 128), F32),
            pltpu.VMEM((3, NZ, 1, 128), F32),
            pltpu.VMEM((3, PLANE, NZ, 1, 128), F32),
            pltpu.VMEM((SLOTS, SLOTS), BF16),
            pltpu.VMEM((SLOTS, HALF), BF16),
            pltpu.VMEM((2, SLOTS, HALF), BF16),
            pltpu.VMEM((FEATURES, SLOTS), BF16),
            pltpu.VMEM((NZ // 2, 512, SLOTS), F32),
            pltpu.VMEM((PARTS, 2, 16, 128), F32),
            pltpu.VMEM((PARTS, 16, 128), F32),
            pltpu.VMEM((2 * PARTS, CHIPS, 16, 128), BF16),
            pltpu.VMEM((2, NZ, 1, 128), F32),
            dma((6,)), dma((2,)), dma((2, PARTS)), dma((2,)), dma((2, PARTS)), dma((3, 4)), dma((5,)), dma((5,)),
            dma((6, 2)), dma((6, 2)), dma((6, 2, 2)), dma((6, 2, 2)),
        ],
        compiler_params=pltpu.CompilerParams(
            collective_id=0, has_side_effects=True, vmem_limit_bytes=63 * 2**20
        ),
    )(
        rows,
        list_ids.reshape(1, ROWS),
        code_ids.reshape(1, ROWS),
        list_slot.reshape(128, 128),
        coarse,
        codebook,
    )
    return updated, nearest.reshape(ROWS)


def solution(mesh):
    placed = (P("rep", "feat"), P("rep"), P("rep"), P(), P("rep", None), P(("rep", "feat"), None))
    return jax.shard_map(
        per_device,
        mesh=mesh,
        in_specs=placed,
        out_specs=(P(("rep", "feat"), None), P("rep")),
        check_vma=False,
    )
```
